32 devices in a mesh: gz: 4 (over y, x), gy: 8 (over z, core).
Axes of the slice: x: 2, y: 2, z: 4, core: 2. Of those that a mesh axis runs over, the one named last changes fastest.
Arguments:
- source: bfloat16 [12, 24, 128, 128], P('gz', 'gy'), may hold values from -6 to 6
- target: bfloat16 [12, 24, 128, 128], P('gz', 'gy'), may hold values from -6 to 6
- hidden: bfloat16 [12, 24, 96, 128], P('gz', 'gy'), may hold values from -1 to 1
- motion: float32 [12, 24, 3, 128], P('gz', 'gy'), may hold values from -6 to 6
- w_corr: bfloat16 [96, 343], replicated, may hold values from -0.3125 to 0.3125
- w_motion: float32 [96, 3], replicated, may hold values from -3.5 to 3.5
- bias_encoder: float32 [96], replicated, may hold values from -3 to 3
- w_update: bfloat16 [27, 18432], replicated, may hold values from -0.078125 to 0.078125
- bias_update: float32 [96], replicated, may hold values from -4 to 4
- w_reset: bfloat16 [27, 18432], replicated, may hold values from -0.078125 to 0.078125
- bias_reset: float32 [96], replicated, may hold values from -4 to 4
- w_cand: bfloat16 [27, 18432], replicated, may hold values from -0.078125 to 0.078125
- bias_cand: float32 [96], replicated, may hold values from -3 to 3
- w_head: bfloat16 [27, 3, 96], replicated, may hold values from -0.125 to 0.125
- bias_head: float32 [3], replicated, may hold values from -3 to 3
Outputs:
- state_out: bfloat16 [12, 24, 96, 128], P('gz', 'gy')
- motion_out: float32 [12, 24, 3, 128], P('gz', 'gy')
The draws below stay inside these ranges and needn't reach their ends.
All inputs are finite; a program needn't handle non-finite values.
Results may differ from the reference program's by a relative error of at most 0.0046.
Values may be sent and summed in bfloat16 or wider, within the bound.
No kernel may reach another device: no remote copies, remote signals or barrier semaphores. Data moves between devices by JAX's collectives and lax.ppermute only.
A program may use at most 64 MiB of HBM per device.

```python
import jax
import jax.numpy as jnp
from jax import lax

FC = 128
HC = 96
OFFSETS = 343
XW = 128
Z = 12
Y = 24


def block_scale(rng, shape, cuts, smallest, high):
    factor_of, own = 1.0, jax.random.fold_in(rng, 6)
    for axis_at, shards_of in cuts:
        steps = jnp.exp(jax.random.uniform(jax.random.fold_in(own, axis_at), (shards_of,), jnp.float32, smallest / len(cuts), high / len(cuts)))
        factor_of = factor_of * jnp.repeat(steps, shape[axis_at] // shards_of).reshape([-1 if axis == axis_at else 1 for axis in range(len(shape))])
    return factor_of


def normal_values(rng, dims, spread, limit, cuts=(), held_as=jnp.bfloat16):
    array = jax.random.normal(rng, dims, jnp.float32) * spread
    if len(cuts) > 0:
        array = block_scale(rng, dims, cuts, -0.22, 0.18) * array
    return jnp.clip(array, min=-limit, max=limit).astype(held_as)


def setup_inputs(seed: int = 0) -> dict:
    arg_keys = jax.random.split(jax.random.key(seed), 16)
    source = normal_values(arg_keys[0], (Z, Y, FC, XW), 1.0, 6.0, ((0, 4), (1, 8)))
    target = normal_values(arg_keys[1], (Z, Y, FC, XW), 1.0, 6.0, ((0, 4), (1, 8)))
    hidden = jnp.clip(jax.random.uniform(arg_keys[2], (Z, Y, HC, XW), jnp.float32, -1.0, 1.0) * block_scale(arg_keys[2], (Z, Y, HC, XW), ((0, 4), (1, 8)), -0.4, 0.0), -1.0, 1.0).astype(jnp.bfloat16)
    motion = normal_values(arg_keys[3], (Z, Y, 3, XW), 1.0, 6.0, ((0, 4), (1, 8)), jnp.float32)
    w_corr = normal_values(arg_keys[4], (HC, OFFSETS), OFFSETS ** -0.5, 0.3125)
    w_motion = normal_values(arg_keys[5], (HC, 3), 3 ** -0.5, 3.5, (), jnp.float32)
    bias_encoder = normal_values(arg_keys[6], (HC,), 0.5, 3.0, (), jnp.float32)
    w_update = normal_values(arg_keys[7], (27, 2 * HC * HC), (54 * HC) ** -0.5, 0.078125)
    bias_update = normal_values(arg_keys[8], (HC,), 1.0, 4.0, (), jnp.float32)
    w_reset = normal_values(arg_keys[9], (27, 2 * HC * HC), (54 * HC) ** -0.5, 0.078125)
    bias_reset = normal_values(arg_keys[10], (HC,), 1.0, 4.0, (), jnp.float32)
    w_cand = normal_values(arg_keys[11], (27, 2 * HC * HC), (54 * HC) ** -0.5, 0.078125)
    bias_cand = normal_values(arg_keys[12], (HC,), 0.5, 3.0, (), jnp.float32)
    w_head = normal_values(arg_keys[13], (27, 3, HC), (27 * HC) ** -0.5, 0.125)
    bias_head = normal_values(arg_keys[14], (3,), 0.5, 3.0, (), jnp.float32)
    return dict(source=source, target=target, hidden=hidden, motion=motion, w_corr=w_corr, w_motion=w_motion, bias_encoder=bias_encoder, w_update=w_update, bias_update=bias_update, w_reset=w_reset, bias_reset=bias_reset, w_cand=w_cand, bias_cand=bias_cand, w_head=w_head, bias_head=bias_head)


def conv_full(field_in, weight):
    if weight.ndim == 2:
        out_width = field_in.shape[2] // 2
        weight = weight.reshape(27, out_width, field_in.shape[2])
    padded = jnp.pad(field_in.astype(jnp.float32), ((1, 1), (1, 1), (0, 0), (1, 1)))
    depth_cells, row_cells = field_in.shape[0], field_in.shape[1]
    col_cells = field_in.shape[3]
    weight_wide = weight.astype(jnp.float32)
    summed = jnp.zeros((depth_cells, row_cells, weight.shape[1], col_cells), jnp.float32)
    for tap_index in range(27):
        depth_off, row_off, col_off = tap_index // 9, (tap_index // 3) % 3, tap_index % 3
        tap_field = padded[depth_off:depth_off + depth_cells, row_off:row_off + row_cells, :, col_off:col_off + col_cells]
        summed = summed + jnp.einsum('oi,zyix->zyox', weight_wide[tap_index], tap_field)
    return summed


def expand(bias_vector):
    return bias_vector[None, None, :, None]


def reference(source, target, hidden, motion, w_corr, w_motion, bias_encoder, w_update, bias_update, w_reset, bias_reset, w_cand, bias_cand, w_head, bias_head):
    depth_cells, row_cells, channels, col_cells = source.shape
    state_width = hidden.shape[2]
    corr_scale = channels ** -0.5
    source_wide = source.astype(jnp.float32)
    padded_target = jnp.pad(target, ((3, 3), (3, 3), (0, 0), (3, 3)))
    zero_index = jnp.zeros((), jnp.int32)

    def one_pair(summed, offset_pair):
        depth_off = (offset_pair // 7).astype(jnp.int32)
        row_off = (offset_pair % 7).astype(jnp.int32)
        target_slab = lax.dynamic_slice(padded_target, (depth_off, row_off, zero_index, zero_index), (depth_cells, row_cells, channels, col_cells + 6))
        planes = []
        for col_off in range(7):
            shifted = target_slab[..., col_off:col_off + col_cells].astype(jnp.float32)
            planes.append(jnp.sum(source_wide * shifted, axis=2) * corr_scale)
        correlation = jnp.stack(planes, 2).astype(jnp.bfloat16)
        weight_block = lax.dynamic_slice_in_dim(w_corr, (offset_pair * 7).astype(jnp.int32), 7, 1)
        summed = summed + jnp.einsum('ok,zykx->zyox', weight_block.astype(jnp.float32), correlation.astype(jnp.float32))
        return summed, None

    start = jnp.zeros((depth_cells, row_cells, w_corr.shape[0], col_cells), jnp.float32)
    summed, _ = lax.scan(one_pair, start, jnp.arange(49, dtype=jnp.int32))
    summed = summed + jnp.einsum('ok,zykx->zyox', w_motion, motion, precision=lax.Precision.HIGHEST)
    encoded = jax.nn.relu(summed + expand(bias_encoder)).astype(jnp.bfloat16)
    joined = jnp.concatenate([hidden, encoded], 2)
    update_gate = jax.nn.sigmoid(conv_full(joined, w_update) + expand(bias_update))
    reset_gate = jax.nn.sigmoid(conv_full(joined, w_reset) + expand(bias_reset))
    gated_state = (reset_gate * hidden).astype(jnp.bfloat16)
    candidate = jnp.tanh(conv_full(jnp.concatenate([gated_state, encoded], 2), w_cand) + expand(bias_cand))
    state_out = ((1.0 - update_gate) * hidden + update_gate * candidate).astype(jnp.bfloat16)
    motion_out = motion + conv_full(state_out, w_head) + expand(bias_head)
    return state_out, motion_out
```

```python
import functools

import jax
import jax.numpy as jnp
from jax import lax
from jax.experimental import pallas as pl
from jax.experimental.pallas import tpu as pltpu
from jax.sharding import PartitionSpec as P

F32 = jnp.float32
BF16 = jnp.bfloat16
LANES = 128
VMEM_LIMIT = 56 * 1024 * 1024


def shift(block, axis, step):
    count = lax.axis_size(axis)
    pairs = [(i, i + step) for i in range(count) if 0 <= i + step < count]
    return lax.ppermute(block, axis, pairs)


def halo(block, axis, dim, width):
    low = shift(lax.slice_in_dim(block, block.shape[dim] - width, None, axis=dim), axis, 1)
    high = shift(lax.slice_in_dim(block, 0, width, axis=dim), axis, -1)
    return low, high


def vmem(count):
    return [pl.BlockSpec(memory_space=pltpu.VMEM)] * count


def call(body, out_shape, scratch, args, flops, name):
    outs = jax.tree.leaves(out_shape)
    moved = sum(a.size * a.dtype.itemsize for a in list(args) + outs)
    return pl.pallas_call(
        body,
        out_shape=out_shape,
        in_specs=vmem(len(args)),
        out_specs=jax.tree.map(lambda _: pl.BlockSpec(memory_space=pltpu.VMEM), out_shape),
        scratch_shapes=scratch,
        compiler_params=pltpu.CompilerParams(vmem_limit_bytes=VMEM_LIMIT),
        cost_estimate=pl.CostEstimate(flops=flops, bytes_accessed=moved, transcendentals=0),
        name=name,
    )(*args)


def prep_body(width, *refs):
    count = (len(refs) - 2) // 2
    ins, outs, flat, wide = refs[:count], refs[count : 2 * count], refs[-2], refs[-1]
    pieces = width * 2 * width // LANES
    half = width // 2
    left = lax.broadcasted_iota(jnp.int32, (half, LANES), 1) < LANES // 2

    for w_ref, o_ref in zip(ins, outs):

        def spread(j, carry):
            got = w_ref[:, pl.ds(pl.multiple_of(j * LANES, LANES), LANES)].astype(F32)
            for first in range(0, 27, 8):
                n = min(8, 27 - first)
                flat[pl.ds(j + first * pieces, n, stride=pieces), :] = got[first : first + n]
            return carry

        lax.fori_loop(0, pieces, spread, 0, unroll=4)

        def tap(ab, c):
            base = (ab * 3 + c) * pieces
            return [flat[pl.ds(base + k, half, stride=3), :] for k in range(3)]

        def put(chunk, c, even, odd):
            wide[chunk, pl.ds(c * width, half, stride=2), :] = even
            wide[chunk, pl.ds(c * width + 1, half, stride=2), :] = odd

        for c in range(3):
            for pair in range(5):
                mids, lasts = [], []
                for ab in range(2 * pair, min(2 * pair + 2, 9)):
                    first, mid, last = tap(ab, c)
                    put(ab, c, first, pltpu.roll(jnp.where(left, last, mid), 64, 1))
                    mids.append(mid)
                    lasts.append(last)
                if len(mids) == 1:
                    zero = jnp.zeros_like(mids[0])
                    even = jnp.where(left, mids[0], zero)
                    odd = jnp.where(left, pltpu.roll(lasts[0], 64, 1), zero)
                else:
                    even = jnp.where(left, mids[0], pltpu.roll(mids[1], 64, 1))
                    odd = jnp.where(left, pltpu.roll(lasts[0], 64, 1), lasts[1])
                put(9 + pair, c, even, odd)
        for chunk in range(14):
            o_ref[:, chunk * LANES : (chunk + 1) * LANES] = wide[chunk].astype(BF16)


def prep_weights(weights, width):
    pieces = width * 2 * width // LANES
    out = jax.ShapeDtypeStruct((3 * width, 14 * LANES), BF16)
    return call(
        functools.partial(prep_body, width),
        (out,) * len(weights),
        [pltpu.VMEM((27 * pieces, LANES), F32), pltpu.VMEM((14, 3 * width, LANES), F32)],
        weights,
        10**9,
        "prep",
    )


def corr_part(js, target_rows, s_flat, tt, corr, wc):
    planes_out, channels, wide = s_flat.shape
    rows_out = wide // LANES
    scale = channels ** (-0.5)
    corr[...] = jnp.zeros_like(corr)
    for at, j in enumerate(js):
        for plane in range(planes_out + 6):
            tt[at, plane] = target_rows(j, plane).T
    sub = lax.broadcasted_iota(jnp.int32, (8, LANES), 0)
    cell = lax.broadcasted_iota(jnp.int32, (8, LANES), 1)
    block_of = (cell + 4 - sub + 8) // 8 - 1

    results = []
    for z in range(planes_out):
        for at, j in enumerate(js):
            ys = [y for y in range(rows_out) if 0 <= j - y <= 6]
            lo, hi = ys[0] * LANES, (ys[-1] + 1) * LANES
            lhs = tt[at, pl.ds(z, 7)].reshape(7 * LANES, channels)
            prod = jnp.dot(lhs, s_flat[z, :, lo:hi], preferred_element_type=F32)
            for a in range(7):
                for n, y in enumerate(ys):
                    got = jnp.zeros((8, LANES), F32)
                    for k in range(LANES // 8):
                        piece = prod[a * LANES + 8 * k : a * LANES + 8 * k + 8, n * LANES : (n + 1) * LANES]
                        got = jnp.where(block_of == k, piece, got)
                    corr[z, a * 7 + j - y, :, y * LANES : (y + 1) * LANES] = got
        turn = (3 - lax.broadcasted_iota(jnp.int32, (1, 8, LANES), 2)) & 7
        turn = jnp.concatenate([turn] * rows_out, axis=2)
        got = corr[z]
        for bit in (1, 2, 4):
            got = jnp.where((turn & bit) != 0, pltpu.roll(got, bit, 1), got)
        got = (got * scale).reshape(49 * 8, wide).astype(BF16)
        results.append(jnp.dot(wc[...], got, preferred_element_type=F32))
    return results


def load_source(source, s_flat):
    for z in range(source.shape[0]):
        for y in range(source.shape[1]):
            s_flat[z, :, y * LANES : (y + 1) * LANES] = source[z, y]


def corr_near_body(source, own, low, high, wc, out, s_flat, tt, corr):
    load_source(source, s_flat)
    planes, rows = own.shape[0], own.shape[1]

    def row(j, plane):
        y = j - 3
        if plane < 3:
            return low[plane, y]
        if plane < 3 + planes:
            return own[plane - 3, y]
        return high[plane - 3 - planes, y]

    for z, got in enumerate(corr_part(range(3, 3 + rows), row, s_flat, tt, corr, wc)):
        out[z] = got


def corr_far_body(source, before, low, high, wc, motion, w_motion, bias, out, s_flat, tt, corr):
    load_source(source, s_flat)
    rows = source.shape[1]

    def row(j, plane):
        return low[plane, j] if j < 3 else high[plane, j - 3 - rows]

    js = list(range(3)) + list(range(3 + rows, 6 + rows))
    for z, got in enumerate(corr_part(js, row, s_flat, tt, corr, wc)):
        for y in range(rows):
            total = got[:, y * LANES : (y + 1) * LANES] + before[z, :, y * LANES : (y + 1) * LANES]
            for k in range(motion.shape[2]):
                total = total + w_motion[:, k : k + 1] * motion[z, y, k : k + 1, :]
            out[z, y] = jnp.maximum(total + bias[...], 0.0).astype(BF16)


def conv(weight, field, planes, z, row, rows):
    wide = rows * LANES
    tops, tails = [], []
    for a in range(3):
        for b in range(3):
            at = slice((row + b) * LANES, (row + b) * LANES + wide)
            tops.append(field[z + a, 0:LANES, at])
            tails.append(field[z + a, LANES:, at])
    rhs = jnp.concatenate(tops + tails + [jnp.zeros((64, wide), BF16)], axis=0)
    three = jnp.dot(weight[...], rhs, preferred_element_type=F32)
    width = three.shape[0] // 3
    cell = lax.broadcasted_iota(jnp.int32, (width, LANES), 1)
    out = []
    for y in range(rows):
        at = slice(y * LANES, (y + 1) * LANES)
        before = jnp.where(cell == 0, 0.0, pltpu.roll(three[:width, at], 1, 1))
        after = jnp.where(cell == LANES - 1, 0.0, pltpu.roll(three[2 * width :, at], LANES - 1, 1))
        out.append(three[width : 2 * width, at] + before + after)
    return out


def gru_body(
    planes, rows, hidden, hz0, hz1, hy0, hy1, enc, ez0, ez1, ey0, ey1, a_up, a_re, a_ca,
    b_up, b_re, b_ca, head, state_out, part_out, joined, gated, state
):
    width = hidden.shape[2]

    def fill(own, z0, z1, y0, y1, first):
        for plane in range(planes + 4):
            for y in range(rows + 4):
                if y < 2:
                    got = y0[plane, y]
                elif y >= rows + 2:
                    got = y1[plane, y - rows - 2]
                elif plane < 2:
                    got = z0[plane, y - 2]
                elif plane >= planes + 2:
                    got = z1[plane - planes - 2, y - 2]
                else:
                    got = own[plane - 2, y - 2]
                joined[plane, first : first + width, y * LANES : (y + 1) * LANES] = got

    fill(hidden, hz0, hz1, hy0, hy1, 0)
    fill(enc, ez0, ez1, ey0, ey1, width)

    def reset_plane(z, carry):
        got = conv(a_re, joined, None, z, 0, rows + 2)
        for y in range(rows + 2):
            at = slice((y + 1) * LANES, (y + 2) * LANES)
            gate = jax.nn.sigmoid(got[y] + b_re[...])
            old = joined[z + 1, 0:width, at].astype(F32)
            to = slice(y * LANES, (y + 1) * LANES)
            gated[z, 0:width, to] = (gate * old).astype(BF16)
            gated[z, width:, to] = joined[z + 1, width:, at]
        return carry

    lax.fori_loop(0, planes + 2, reset_plane, 0)

    def state_plane(z, carry):
        update = conv(a_up, joined, None, z + 1, 1, rows)
        cand = conv(a_ca, gated, None, z, 0, rows)
        for y in range(rows):
            gate = jax.nn.sigmoid(update[y] + b_up[...])
            new = jnp.tanh(cand[y] + b_ca[...])
            old = hidden[z, y].astype(F32)
            got = ((1.0 - gate) * old + gate * new).astype(BF16)
            state_out[z, y] = got
            state[z, :, y * LANES : (y + 1) * LANES] = got
        return carry

    lax.fori_loop(0, planes, state_plane, 0)

    cell = lax.broadcasted_iota(jnp.int32, (8, LANES), 1)
    sums = {}
    for z in range(planes):
        prod = jnp.dot(head[...], state[z], preferred_element_type=F32)
        for y in range(rows):
            for a in range(3):
                for b in range(3):
                    key = (z + 2 - a, y + 2 - b)
                    for c in range(3):
                        t = a * 9 + b * 3 + c
                        piece = prod[t * 8 : t * 8 + 8, y * LANES : (y + 1) * LANES]
                        slot = sums.setdefault(key, [None] * 3)
                        slot[c] = piece if slot[c] is None else slot[c] + piece
    for (z, y), (before, same, after) in sums.items():
        before = jnp.where(cell == 0, 0.0, pltpu.roll(before, 1, 1))
        after = jnp.where(cell == LANES - 1, 0.0, pltpu.roll(after, LANES - 1, 1))
        part_out[z, y] = same + before + after


def on_device(
    source, target, hidden, motion, w_corr, w_motion, bias_encoder, w_update, bias_update,
    w_reset, bias_reset, w_cand, bias_cand, w_head, bias_head
):
    planes, rows, channels, cells = source.shape
    width = hidden.shape[2]
    wide = rows * LANES

    t_low, t_high = halo(target, "gz", 0, 3)
    tall = jnp.concatenate([t_low, target, t_high], axis=0)
    t_left, t_right = halo(tall, "gy", 1, 3)

    h_low, h_high = halo(hidden, "gz", 0, 2)
    h_tall = jnp.concatenate([h_low, hidden, h_high], axis=0)
    h_left, h_right = halo(h_tall, "gy", 1, 2)

    a_up, a_re, a_ca = prep_weights((w_update, w_reset, w_cand), width)
    wc = jnp.pad(w_corr.reshape(width, 49, 7), ((0, 0), (0, 0), (0, 1))).reshape(width, 49 * 8)
    head = jnp.pad(w_head, ((0, 0), (0, 8 - w_head.shape[1]), (0, 0))).reshape(27 * 8, width)

    def corr_scratch(js):
        return [
            pltpu.VMEM((planes, channels, wide), BF16),
            pltpu.VMEM((js, planes + 6, LANES, channels), BF16),
            pltpu.VMEM((planes, 49, 8, wide), F32),
        ]

    near = call(
        corr_near_body,
        jax.ShapeDtypeStruct((planes, width, wide), F32),
        corr_scratch(rows),
        (source, target, t_low, t_high, wc),
        10**9,
        "near",
    )
    enc = call(
        corr_far_body,
        jax.ShapeDtypeStruct((planes, rows, width, cells), BF16),
        corr_scratch(6),
        (source, near, t_left, t_right, wc, motion, w_motion, bias_encoder[:, None]),
        10**9,
        "far",
    )
    e_low, e_high = halo(enc, "gz", 0, 2)
    e_tall = jnp.concatenate([e_low, enc, e_high], axis=0)
    e_left, e_right = halo(e_tall, "gy", 1, 2)

    state_out, part = call(
        functools.partial(gru_body, planes, rows),
        (
            jax.ShapeDtypeStruct((planes, rows, width, cells), BF16),
            jax.ShapeDtypeStruct((planes + 2, rows + 2, 8, cells), F32),
        ),
        [
            pltpu.VMEM((planes + 4, 2 * width, (rows + 4) * LANES), BF16),
            pltpu.VMEM((planes + 2, 2 * width, (rows + 2) * LANES), BF16),
            pltpu.VMEM((planes, width, wide), BF16),
        ],
        (hidden, h_low, h_high, h_left, h_right, enc, e_low, e_high, e_left, e_right, a_up, a_re, a_ca)
        + (bias_update[:, None], bias_reset[:, None], bias_cand[:, None], head),
        4 * 10**9,
        "gru",
    )
    from_low, from_high = shift(part[-1:], "gz", 1), shift(part[:1], "gz", -1)
    mine = part[1:-1]
    mine = jnp.concatenate([mine[:1] + from_low, mine[1:-1], mine[-1:] + from_high], axis=0)
    from_left, from_right = shift(mine[:, -1:], "gy", 1), shift(mine[:, :1], "gy", -1)
    mine = mine[:, 1:-1]
    mine = jnp.concatenate([mine[:, :1] + from_left, mine[:, 1:-1], mine[:, -1:] + from_right], axis=1)
    outs = motion.shape[2]
    motion_out = motion + mine[:, :, :outs] + bias_head[None, None, :, None]
    return state_out, motion_out


def solution(mesh):
    split = P("gz", "gy", None, None)
    return jax.shard_map(
        on_device,
        mesh=mesh,
        in_specs=(split,) * 4 + (P(),) * 11,
        out_specs=(split, split),
        check_vma=False,
    )
```

```python
import functools

import jax
import jax.numpy as jnp
from jax import lax
from jax.experimental import pallas as pl
from jax.experimental.pallas import tpu as pltpu
from jax.sharding import PartitionSpec as P

F32 = jnp.float32
BF16 = jnp.bfloat16
LANES = 128
MIB = 1024 * 1024


def around(block, axis, step):
    count = lax.axis_size(axis)
    return lax.ppermute(block, axis, [(i, (i + step) % count) for i in range(count)])


def planes_around(first, last):
    return around(last, "gz", 1), around(first, "gz", -1)


def rows_around(to_mate, to_other):
    count = lax.axis_size("gy")
    mate = lax.ppermute(to_mate, "gy", [(i, i ^ 1) for i in range(count)])
    other = lax.ppermute(to_other, "gy", [(i, ((i + 1) ^ 1) - 1) for i in range(1, count - 1)])
    return mate, other


def edges(block, width):
    rows = block.shape[1]
    if rows == width:
        return block, block
    odd = lax.axis_index("gy") % 2
    to_mate = lax.dynamic_slice_in_dim(block, (rows - width) * (1 - odd), width, axis=1)
    return to_mate, lax.dynamic_slice_in_dim(block, (rows - width) * odd, width, axis=1)


def inside():
    z, y = lax.axis_index("gz"), lax.axis_index("gy")
    odd = y % 2
    end = jnp.where(odd == 1, lax.axis_size("gy") - 1, 0)
    return jnp.stack([z > 0, z < lax.axis_size("gz") - 1, y != end, odd == 1]).astype(jnp.int32)


def vmem(count):
    return [pl.BlockSpec(memory_space=pltpu.VMEM)] * count


def call(body, out_shape, scratch, args, name, mib, place=None, from_hbm=(), kept=True):
    struct = lambda o: isinstance(o, jax.ShapeDtypeStruct)
    in_specs = vmem(len(args))
    for n, given in enumerate(from_hbm):
        in_specs[n] = pl.BlockSpec(memory_space=given)
    args = [pltpu.with_memory_space_constraint(a, pltpu.HBM if n < len(from_hbm) else pltpu.VMEM) for n, a in enumerate(args)]
    if place is not None:
        args = [place] + args
        in_specs = [pl.BlockSpec(memory_space=pltpu.SMEM)] + in_specs
    return pl.pallas_call(
        body,
        out_shape=jax.tree.map(lambda o: pltpu.VMEM(o.shape, o.dtype) if kept and struct(o) else o, out_shape),
        in_specs=in_specs,
        out_specs=jax.tree.map(lambda _: pl.BlockSpec(memory_space=pltpu.VMEM), out_shape),
        scratch_shapes=scratch,
        compiler_params=pltpu.CompilerParams(vmem_limit_bytes=mib * MIB),
        cost_estimate=pl.CostEstimate(flops=1000, bytes_accessed=1000, transcendentals=0),
        name=name,
    )(*args)


def lay_out(width, weight, first_out, last_out, flat, wide):
    pieces = width * 2 * width // LANES
    half = width // 2
    lane = lax.broadcasted_iota(jnp.int32, (half, LANES), 1)

    def turn(value, by):
        return pltpu.roll(value, by, 1)

    def packed(parts):
        made = []
        for first in range(0, 9, 4):
            group = parts[first : first + 4]
            if len(group) == 1:
                made.append(jnp.where(lane < 96, group[0], 0.0))
                continue
            one, two = turn(group[1], 96), turn(group[2], 64)
            made.append(jnp.where(lane < 96, group[0], one))
            made.append(jnp.where(lane < 64, one, two))
            made.append(jnp.where(lane < 32, two, turn(group[3], 32)))
        return made

    def spread(j, carry):
        got = weight[:, pl.ds(pl.multiple_of(j * LANES, LANES), LANES)].astype(F32)
        for first in range(0, 27, 8):
            size = min(8, 27 - first)
            flat[pl.ds(j + first * pieces, size, stride=pieces), :] = got[first : first + size]
        return carry

    lax.fori_loop(0, pieces, spread, 0, unroll=4)

    for c in range(3):
        rows = [[], [], [], []]
        for ab in range(9):
            first, mid, last = [flat[pl.ds((ab * 3 + c) * pieces + k, half, stride=3), :] for k in range(3)]
            rows[0].append(first)
            rows[1].append(turn(jnp.where(lane < 64, last, mid), 64))
            rows[2].append(turn(jnp.where(lane >= 96, first, mid), 32))
            rows[3].append(turn(last, 96))
        for part in range(4):
            for k, chunk in enumerate(packed(rows[part])):
                wide[part // 2, k, pl.ds(c * width + part % 2, half, stride=2), :] = chunk
    for part, out in enumerate((first_out, last_out)):
        for chunk in range(7):
            out[:, chunk * LANES : (chunk + 1) * LANES] = wide[part, chunk].astype(BF16)


def lay_out_scratch(width):
    return [pltpu.VMEM((27 * width * 2 * width // LANES, LANES), F32), pltpu.VMEM((2, 7, 3 * width, LANES), F32)]


def update_body(weight, first_out, last_out, flat, wide):
    lay_out(first_out.shape[0] // 3, weight, first_out, last_out, flat, wide)


def cand_body(weight, head, first_out, last_out, head_out, flat, wide, eights):
    width = head.shape[2]
    lay_out(width, weight, first_out, last_out, flat, wide)
    eights[...] = jnp.zeros_like(eights)
    for o in range(head.shape[0]):
        eights[pl.ds(o, 27, stride=8), :width] = head[o].astype(F32)
    head_out[...] = eights[:, :width].astype(BF16)


def corr_part(held, source, tt, s_flat, corr, wc):
    planes_out, rows_out, channels, _ = source.shape
    wide = rows_out * LANES
    scale = channels ** (-0.5)
    for z in range(planes_out):
        for y in range(rows_out):
            s_flat[z, :, y * LANES : (y + 1) * LANES] = source[z, y]
    sub = lax.broadcasted_iota(jnp.int32, (8, LANES), 0)
    cell = lax.broadcasted_iota(jnp.int32, (8, LANES), 1)
    block_of = (cell + 4 - sub + 8) // 8 - 1
    turn = (3 - lax.broadcasted_iota(jnp.int32, (1, 8, LANES), 2)) & 7
    turn = jnp.concatenate([turn] * rows_out, axis=2)

    results = []
    for z in range(planes_out):
        filled = set()
        for j in range(rows_out + 6):
            ys = [y for y in range(rows_out) if 0 <= j - y <= 6]
            lo, hi = ys[0] * LANES, (ys[-1] + 1) * LANES
            for first, last in held(j):
                first, last = max(z, first), min(z + 7, last)
                if first >= last:
                    continue
                lhs = tt[j, first:last].reshape((last - first) * LANES, channels)
                prod = jnp.dot(lhs, s_flat[z, :, lo:hi], preferred_element_type=F32)
                for plane in range(first, last):
                    for n, y in enumerate(ys):
                        got = jnp.zeros((8, LANES), F32)
                        for k in range(LANES // 8):
                            at = (plane - first) * LANES + 8 * k
                            piece = prod[at : at + 8, n * LANES : (n + 1) * LANES]
                            got = jnp.where(block_of == k, piece, got)
                        corr[(plane - z) * 7 + j - y, :, y * LANES : (y + 1) * LANES] = got
                        filled.add(((plane - z) * 7 + j - y, y))
        for pair in range(49):
            for y in range(rows_out):
                if (pair, y) not in filled:
                    corr[pair, :, y * LANES : (y + 1) * LANES] = jnp.zeros((8, LANES), F32)
        got = corr[...]
        for bit in (1, 2, 4):
            got = jnp.where((turn & bit) != 0, pltpu.roll(got, bit, 1), got)
        got = (got * scale).reshape(49 * 8, wide).astype(BF16)
        results.append(jnp.dot(wc[...], got, preferred_element_type=F32))
    return results


def put_block(tt, block, ok, row, plane):
    def store(value):
        for p in range(block.shape[0]):
            for y in range(block.shape[1]):
                tt[row + y, plane + p] = value(p, y)

    if ok is None:
        store(lambda p, y: block[p, y].T)
        return

    @pl.when(ok)
    def _():
        store(lambda p, y: block[p, y].T)

    @pl.when(jnp.logical_not(ok))
    def _():
        store(lambda p, y: jnp.zeros(tt.shape[2:], BF16))


def column(row):
    return jnp.broadcast_to(row, (LANES, row.shape[1])).T


def own_body(
    w_reset, w_update, source, own, w_corr, hidden,
    out, wc, h_first, h_last, re_old, re_new, update_here, tt, s_flat, corr, reset_here, flat, wide, arrived
):
    copies = [
        pltpu.make_async_copy(w_reset, reset_here, arrived.at[0]),
        pltpu.make_async_copy(w_update, update_here, arrived.at[1]),
    ]
    for copy in copies:
        copy.start()
    planes, rows = source.shape[:2]
    h_first[...] = hidden[:2]
    h_last[...] = hidden[planes - 2 :]
    at = lax.broadcasted_iota(jnp.int32, (w_corr.shape[1], 49 * 8), 0)
    to = lax.broadcasted_iota(jnp.int32, (w_corr.shape[1], 49 * 8), 1)
    pick = ((to & 7) < 7) & (at == (to >> 3) * 7 + (to & 7))
    wc[...] = jnp.dot(w_corr[...], jnp.where(pick, 1.0, 0.0).astype(BF16), preferred_element_type=F32).astype(BF16)
    put_block(tt, own, None, 3, 3)
    held = lambda j: [(3, 3 + planes)] if 3 <= j < 3 + rows else []
    for z, got in enumerate(corr_part(held, source, tt, s_flat, corr, wc)):
        out[z] = got
    copies[0].wait()
    lay_out(hidden.shape[2], reset_here, re_old, re_new, flat, wide)
    copies[1].wait()


def corr_face_body(place, source, before, low, high, mate, other, wc, out, tt, s_flat, corr):
    planes, rows = source.shape[:2]
    odd = place[3]
    put_block(tt, low, place[0] == 1, 3, 0)
    put_block(tt, high, place[1] == 1, 3, 3 + planes)
    put_block(tt, mate, None, (3 + rows) * (1 - odd), 3)
    put_block(tt, other, place[2] == 1, (3 + rows) * odd, 3)

    def held(j):
        return [(3, 3 + planes)] if j < 3 or j >= 3 + rows else [(0, 3), (3 + planes, 6 + planes)]

    for z, got in enumerate(corr_part(held, source, tt, s_flat, corr, wc)):
        out[z] = before[z] + got


def corr_corner_body(
    place, source, motion, w_motion, bias, before, low_mate, low_other, high_mate, high_other, wc,
    enc, enc_first, enc_last, tt, s_flat, corr
):
    planes, rows = source.shape[:2]
    odd = place[3]
    mate_at, other_at = (3 + rows) * (1 - odd), (3 + rows) * odd
    put_block(tt, low_mate, place[0] == 1, mate_at, 0)
    put_block(tt, low_other, place[0] + place[2] == 2, other_at, 0)
    put_block(tt, high_mate, place[1] == 1, mate_at, 3 + planes)
    put_block(tt, high_other, place[1] + place[2] == 2, other_at, 3 + planes)
    held = lambda j: [(0, 3), (3 + planes, 6 + planes)] if j < 3 or j >= 3 + rows else []
    shift = column(bias[...])
    moves = [column(w_motion[k : k + 1, :]) for k in range(w_motion.shape[0])]
    for z, got in enumerate(corr_part(held, source, tt, s_flat, corr, wc)):
        for y in range(rows):
            at = slice(y * LANES, (y + 1) * LANES)
            total = got[:, at] + before[z, :, at]
            for k, move in enumerate(moves):
                total = total + move * motion[z, y, k : k + 1, :]
            value = jnp.maximum(total + shift, 0.0).astype(BF16)
            enc[z, y] = value
            if z < 2:
                enc_first[z, y] = value
            if z >= planes - 2:
                enc_last[z - planes + 2, y] = value


def pack_body(place, own, low, high, to_mate, to_other):
    width = to_mate.shape[1]
    planes, rows = own.shape[:2]
    odd = place[3]
    for y in range(width):
        mate_at, other_at = (rows - width) * (1 - odd) + y, (rows - width) * odd + y
        first = 0
        for block in (low, own, high):
            to_mate[first : first + block.shape[0], y] = block[:, mate_at]
            to_other[first : first + block.shape[0], y] = block[:, other_at]
            first += block.shape[0]


def rows_of(place, low, own, high, width, name, from_hbm=()):
    planes = low.shape[0] + own.shape[0] + high.shape[0]
    out = jax.ShapeDtypeStruct((planes, width) + own.shape[2:], own.dtype)
    return call(pack_body, (out, out), [], (own, low, high), name, 6, place, from_hbm)


def taps(field, z, row, rows):
    wide = rows * LANES
    got = []
    for a in range(3):
        for b in range(3):
            got.append(field[z + a, :, (row + b) * LANES : (row + b) * LANES + wide])
    return got + [jnp.zeros((32, wide), BF16)]


def conv(weight, rhs, rows):
    three = jnp.dot(weight, jnp.concatenate(rhs, axis=0), preferred_element_type=F32)
    width = three.shape[0] // 3
    cell = lax.broadcasted_iota(jnp.int32, (width, LANES), 1)
    out = []
    for y in range(rows):
        at = slice(y * LANES, (y + 1) * LANES)
        before = jnp.where(cell == 0, 0.0, pltpu.roll(three[:width, at], 1, 1))
        after = jnp.where(cell == LANES - 1, 0.0, pltpu.roll(three[2 * width :, at], LANES - 1, 1))
        out.append(three[width : 2 * width, at] + before + after)
    return out


def fill(place, field, own, z0, z1, mate, other):
    planes, rows, width = own.shape[:3]
    odd = place[3]

    def store(plane, y, value):
        at = y * LANES if isinstance(y, int) else pl.multiple_of(y * LANES, LANES)
        field[plane, :, pl.ds(at, LANES)] = value

    def store_if(ok, plane, y, value):
        @pl.when(ok)
        def _():
            store(plane, y, value())

        @pl.when(jnp.logical_not(ok))
        def _():
            store(plane, y, jnp.zeros((width, LANES), BF16))

    for plane in range(planes + 4):
        in_z = None
        if plane < 2:
            in_z = place[0]
        elif plane >= planes + 2:
            in_z = place[1]
        for y in range(rows):
            if plane < 2:
                store_if(in_z == 1, plane, y + 2, lambda: z0[plane, y])
            elif plane >= planes + 2:
                store_if(in_z == 1, plane, y + 2, lambda: z1[plane - planes - 2, y])
            else:
                store(plane, y + 2, own[plane - 2, y])
        for y in range(2):
            mate_at, other_at = y + (rows + 2) * (1 - odd), y + (rows + 2) * odd
            if in_z is None:
                store(plane, mate_at, mate[plane, y])
                store_if(place[2] == 1, plane, other_at, lambda: other[plane, y])
            else:
                store_if(in_z == 1, plane, mate_at, lambda: mate[plane, y])
                store_if(in_z + place[2] == 2, plane, other_at, lambda: other[plane, y])


def old_body(place, hidden, b_up, b_re, hz0, hz1, h_mate, h_other, a_up, a_re, update_out, reset_out, near_out, field):
    planes, rows = hidden.shape[:2]
    fill(place, field, hidden, hz0, hz1, h_mate, h_other)
    up_shift, re_shift = column(b_up[...]), column(b_re[...])

    def reset_plane(z, carry):
        near_out[z] = field[z + 1, :, LANES : (rows + 3) * LANES]
        for y, got in enumerate(conv(a_re[...], taps(field, z, 0, rows + 2), rows + 2)):
            reset_out[z, y] = got + re_shift
        return carry

    lax.fori_loop(0, planes + 2, reset_plane, 0)

    def update_plane(z, carry):
        for y, got in enumerate(conv(a_up[...], taps(field, z + 1, 1, rows), rows)):
            update_out[z, y] = got + up_shift
        return carry

    lax.fori_loop(0, planes, update_plane, 0)


def gru_body(
    place, hidden, b_ca, near, update_old, reset_old, enc, ez0, ez1, e_mate, e_other, a_up, a_re, a_ca_old, a_ca_new,
    head, state_out, part_low, part_out, part_high, field, gated, state
):
    planes, rows = hidden.shape[:2]
    fill(place, field, enc, ez0, ez1, e_mate, e_other)
    ca_shift = column(b_ca[...])

    def reset_plane(z, carry):
        for y, got in enumerate(conv(a_re[...], taps(field, z, 0, rows + 2), rows + 2)):
            at = slice(y * LANES, (y + 1) * LANES)
            gate = jax.nn.sigmoid(got + reset_old[z, y])
            gated[z, :, at] = (gate * near[z, :, at].astype(F32)).astype(BF16)
        return carry

    lax.fori_loop(0, planes + 2, reset_plane, 0)

    def state_plane(z, carry):
        new_taps = taps(field, z + 1, 1, rows)
        update = conv(a_up[...], new_taps, rows)
        both = jnp.concatenate([a_ca_old[...], a_ca_new[...]], axis=1)
        cand = conv(both, taps(gated, z, 0, rows) + new_taps, rows)
        for y in range(rows):
            gate = jax.nn.sigmoid(update[y] + update_old[z, y])
            new = jnp.tanh(cand[y] + ca_shift)
            old = hidden[z, y].astype(F32)
            got = ((1.0 - gate) * old + gate * new).astype(BF16)
            state_out[z, y] = got
            state[z, :, y * LANES : (y + 1) * LANES] = got
        return carry

    lax.fori_loop(0, planes, state_plane, 0)

    cell = lax.broadcasted_iota(jnp.int32, (8, LANES), 1)
    sums = {}
    for z in range(planes):
        prod = jnp.dot(head[...], state[z], preferred_element_type=F32)
        for y in range(rows):
            for a in range(3):
                for b in range(3):
                    key = (z + 2 - a, y + 2 - b)
                    for c in range(3):
                        t = a * 9 + b * 3 + c
                        piece = prod[t * 8 : t * 8 + 8, y * LANES : (y + 1) * LANES]
                        slot = sums.setdefault(key, [None] * 3)
                        slot[c] = piece if slot[c] is None else slot[c] + piece
    for (z, y), (before, same, after) in sums.items():
        before = jnp.where(cell == 0, 0.0, pltpu.roll(before, 1, 1))
        after = jnp.where(cell == LANES - 1, 0.0, pltpu.roll(after, LANES - 1, 1))
        total = same + before + after
        if z == 0:
            part_low[0, y] = total
        elif z == planes + 1:
            part_high[0, y] = total
        else:
            part_out[z - 1, y] = total


def mix_body(place, part, low, high, mine, to_mate, to_other):
    planes, rows = mine.shape[:2]
    odd = place[3]
    mate_at, other_at = (rows + 1) * (1 - odd), (rows + 1) * odd

    def added(z, at):
        total = part[z, at]
        if z == 0:
            total = total + jnp.where(place[0] == 1, low[0, at], 0.0)
        if z == planes - 1:
            total = total + jnp.where(place[1] == 1, high[0, at], 0.0)
        return total

    for z in range(planes):
        for y in range(rows):
            mine[z, y] = added(z, y + 1)
        to_mate[z, 0] = added(z, mate_at)
        to_other[z, 0] = added(z, other_at)


def last_body(place, motion, bias, mine, mate, other, out):
    planes, rows, outs = out.shape[:3]
    odd = place[3]
    shift = column(bias[...])
    for z in range(planes):
        for y in range(rows):
            out[z, y] = motion[z, y] + mine[z, y, :outs] + shift
        mate_at, other_at = (rows - 1) * (1 - odd), (rows - 1) * odd
        out[z, mate_at] = out[z, mate_at] + mate[z, 0, :outs]

        @pl.when(place[2] == 1)
        def _():
            out[z, other_at] = out[z, other_at] + other[z, 0, :outs]


def on_device(
    source, target, hidden, motion, w_corr, w_motion, bias_encoder, w_update, bias_update,
    w_reset, bias_reset, w_cand, bias_cand, w_head, bias_head
):
    planes, rows, channels, cells = source.shape
    width = hidden.shape[2]
    wide = rows * LANES
    place = inside()

    t_low, t_high = planes_around(target[:3], target[-3:])
    t_mate, t_other = rows_around(*edges(target, 3))

    scratch = [
        pltpu.VMEM((rows + 6, planes + 6, LANES, channels), BF16),
        pltpu.VMEM((planes, channels, wide), BF16),
        pltpu.VMEM((49, 8, wide), F32),
    ]
    sums = jax.ShapeDtypeStruct((planes, width, wide), F32)
    two = jax.ShapeDtypeStruct((2, rows, width, cells), BF16)
    laid = pltpu.HBM((3 * width, 7 * LANES), BF16)
    own, wc, h_first, h_last, re_old, re_new, update_here = call(
        own_body,
        (sums, jax.ShapeDtypeStruct((width, 49 * 8), BF16), two, two, laid, laid)
        + (jax.ShapeDtypeStruct(w_update.shape, BF16),),
        scratch + [pltpu.VMEM(w_reset.shape, BF16)] + lay_out_scratch(width) + [pltpu.SemaphoreType.DMA((2,))],
        (w_reset, w_update, source, target, w_corr, hidden),
        "own",
        20,
        from_hbm=(pltpu.HBM,) * 2 + (pltpu.VMEM,) * 4,
    )
    t_low, own = lax.optimization_barrier((t_low, own))
    t_low_mate, t_low_other = rows_around(*edges(t_low, 3))
    update_here, t_low = lax.optimization_barrier((update_here, t_low))
    up_old, up_new = call(
        update_body, (laid, laid), lay_out_scratch(width), (update_here,), "lay_out_update", 12
    )
    t_high, up_new = lax.optimization_barrier((t_high, up_new))
    t_high_mate, t_high_other = rows_around(*edges(t_high, 3))
    h_first, h_last, t_low, t_high = lax.optimization_barrier((h_first, h_last, t_low, t_high))
    h_low, h_high = planes_around(h_first, h_last)
    face = call(
        corr_face_body, sums, scratch, (source, own, t_low, t_high, t_mate, t_other, wc), "face", 12, place,
        from_hbm=(pltpu.VMEM,),
    )
    enc, enc_first, enc_last = call(
        corr_corner_body,
        (jax.ShapeDtypeStruct((planes, rows, width, cells), BF16), two, two),
        scratch,
        (source, motion, w_motion.T, bias_encoder[None, :])
        + (face, t_low_mate, t_low_other, t_high_mate, t_high_other, wc),
        "corner",
        12,
        place,
        from_hbm=(pltpu.VMEM,) * 4,
    )
    e_low, e_high = planes_around(enc_first, enc_last)
    taps_head, enc = lax.optimization_barrier((jnp.transpose(w_head, (1, 0, 2)), enc))
    ca_old, ca_new, head = call(
        cand_body,
        (laid, laid, pltpu.HBM((27 * 8, width), BF16)),
        lay_out_scratch(width) + [pltpu.VMEM((27 * 8, LANES), F32)],
        (w_cand, taps_head),
        "lay_out_cand",
        12,
        from_hbm=(pltpu.VMEM,) * 2,
    )
    e_low, ca_new = lax.optimization_barrier((e_low, ca_new))
    h_low, h_high, enc = lax.optimization_barrier((h_low, h_high, enc))
    h_mate, h_other = rows_around(*rows_of(place, h_low, hidden, h_high, 2, "pack_hidden", (pltpu.VMEM,)))
    field = pltpu.VMEM((planes + 4, width, (rows + 4) * LANES), BF16)
    update_old, reset_old, near = call(
        old_body,
        (
            jax.ShapeDtypeStruct((planes, rows, width, cells), F32),
            jax.ShapeDtypeStruct((planes + 2, rows + 2, width, cells), F32),
            jax.ShapeDtypeStruct((planes + 2, width, (rows + 2) * LANES), BF16),
        ),
        [field],
        (hidden, bias_update[None, :], bias_reset[None, :], h_low, h_high, h_mate, h_other, up_old, re_old),
        "old",
        12,
        place,
        from_hbm=(pltpu.VMEM,) * 3,
    )
    e_mate, e_other = rows_around(*rows_of(place, e_low, enc, e_high, 2, "pack_encoded"))

    ring = lambda n: jax.ShapeDtypeStruct((n, rows + 2, 8, cells), F32)
    state_out, part_low, part, part_high = call(
        gru_body,
        (jax.ShapeDtypeStruct((planes, rows, width, cells), BF16), ring(1), ring(planes), ring(1)),
        [
            field,
            pltpu.VMEM((planes + 2, width, (rows + 2) * LANES), BF16),
            pltpu.VMEM((planes, width, wide), BF16),
        ],
        (hidden, bias_cand[None, :], near, update_old, reset_old, enc, e_low, e_high, e_mate, e_other)
        + (up_new, re_new, ca_old, ca_new, head),
        "gru",
        14,
        place,
        from_hbm=(pltpu.VMEM,) * 2,
        kept=False,
    )
    low, high = planes_around(part_low, part_high)
    row = jax.ShapeDtypeStruct((planes, 1, 8, cells), F32)
    mine, to_mate, to_other = call(
        mix_body,
        (jax.ShapeDtypeStruct((planes, rows, 8, cells), F32), row, row),
        [],
        (part, low, high),
        "mix",
        4,
        place,
    )
    mate, other = rows_around(to_mate, to_other)
    motion_out = call(
        last_body,
        jax.ShapeDtypeStruct(motion.shape, F32),
        [],
        (motion, bias_head[None, :], mine, mate, other),
        "last",
        4,
        place,
        from_hbm=(pltpu.VMEM,) * 2,
        kept=False,
    )
    return state_out, motion_out


def solution(mesh):
    split = P("gz", "gy", None, None)
    return jax.shard_map(
        on_device,
        mesh=mesh,
        in_specs=(split,) * 4 + (P(),) * 11,
        out_specs=(split, split),
        check_vma=False,
    )
```

```python
import functools

import jax
import jax.numpy as jnp
from jax import lax
from jax.experimental import pallas as pl
from jax.experimental.pallas import tpu as pltpu
from jax.sharding import PartitionSpec as P

F32 = jnp.float32
BF16 = jnp.bfloat16
LANES = 128
MIB = 1024 * 1024


def around(block, axis, step):
    count = lax.axis_size(axis)
    return lax.ppermute(block, axis, [(i, (i + step) % count) for i in range(count)])


def planes_around(first, last):
    return around(last, "gz", 1), around(first, "gz", -1)


def rows_around(to_mate, to_other):
    count = lax.axis_size("gy")
    mate = lax.ppermute(to_mate, "gy", [(i, i ^ 1) for i in range(count)])
    other = lax.ppermute(to_other, "gy", [(i, ((i + 1) ^ 1) - 1) for i in range(1, count - 1)])
    return mate, other


def edges(block, width):
    rows = block.shape[1]
    if rows == width:
        return block, block
    odd = lax.axis_index("gy") % 2
    to_mate = lax.dynamic_slice_in_dim(block, (rows - width) * (1 - odd), width, axis=1)
    return to_mate, lax.dynamic_slice_in_dim(block, (rows - width) * odd, width, axis=1)


def inside():
    z, y = lax.axis_index("gz"), lax.axis_index("gy")
    odd = y % 2
    end = jnp.where(odd == 1, lax.axis_size("gy") - 1, 0)
    return jnp.stack([z > 0, z < lax.axis_size("gz") - 1, y != end, odd == 1]).astype(jnp.int32)


def vmem(count):
    return [pl.BlockSpec(memory_space=pltpu.VMEM)] * count


def call(body, out_shape, scratch, args, name, mib, place=None, from_hbm=(), kept=True):
    struct = lambda o: isinstance(o, jax.ShapeDtypeStruct)
    in_specs = vmem(len(args))
    for n, given in enumerate(from_hbm):
        in_specs[n] = pl.BlockSpec(memory_space=given)
    args = [pltpu.with_memory_space_constraint(a, pltpu.HBM if n < len(from_hbm) else pltpu.VMEM) for n, a in enumerate(args)]
    if place is not None:
        args = [place] + args
        in_specs = [pl.BlockSpec(memory_space=pltpu.SMEM)] + in_specs
    return pl.pallas_call(
        body,
        out_shape=jax.tree.map(lambda o: pltpu.VMEM(o.shape, o.dtype) if kept and struct(o) else o, out_shape),
        in_specs=in_specs,
        out_specs=jax.tree.map(lambda _: pl.BlockSpec(memory_space=pltpu.VMEM), out_shape),
        scratch_shapes=scratch,
        compiler_params=pltpu.CompilerParams(vmem_limit_bytes=mib * MIB),
        cost_estimate=pl.CostEstimate(flops=1000, bytes_accessed=1000, transcendentals=0),
        name=name,
    )(*args)


def lay_out(width, weight, first_out, last_out, flat, wide):
    pieces = width * 2 * width // LANES
    pitch = pieces + 1
    half = width // 2
    lane = lax.broadcasted_iota(jnp.int32, (half, LANES), 1)

    def turn(value, by):
        return pltpu.roll(value, by, 1)

    def packed(parts):
        made = []
        for first in range(0, 9, 4):
            group = parts[first : first + 4]
            if len(group) == 1:
                made.append(jnp.where(lane < 96, group[0], 0.0))
                continue
            one, two = turn(group[1], 96), turn(group[2], 64)
            made.append(jnp.where(lane < 96, group[0], one))
            made.append(jnp.where(lane < 64, one, two))
            made.append(jnp.where(lane < 32, two, turn(group[3], 32)))
        return made

    def spread(j, carry):
        got = weight[:, pl.ds(pl.multiple_of(j * LANES, LANES), LANES)].astype(F32)
        for first in range(0, 27, 8):
            size = min(8, 27 - first)
            flat[pl.ds(j + first * pitch, size, stride=pitch), :] = got[first : first + size]
        return carry

    lax.fori_loop(0, pieces, spread, 0, unroll=8)

    for c in range(3):
        rows = [[], [], [], []]
        for ab in range(9):
            first, mid, last = [flat[pl.ds((ab * 3 + c) * pitch + k, half, stride=3), :] for k in range(3)]
            rows[0].append(first)
            rows[1].append(turn(jnp.where(lane < 64, last, mid), 64))
            rows[2].append(turn(jnp.where(lane >= 96, first, mid), 32))
            rows[3].append(turn(last, 96))
        for part in range(4):
            for k, chunk in enumerate(packed(rows[part])):
                wide[part // 2, k, pl.ds(c * width + part % 2, half, stride=2), :] = chunk
    for part, out in enumerate((first_out, last_out)):
        for chunk in range(7):
            out[:, chunk * LANES : (chunk + 1) * LANES] = wide[part, chunk].astype(BF16)


def lay_out_scratch(width):
    pitch = width * 2 * width // LANES + 1
    return [pltpu.VMEM((27 * pitch, LANES), F32), pltpu.VMEM((2, 7, 3 * width, LANES), F32)]


def update_body(weight, first_out, last_out, flat, wide):
    lay_out(first_out.shape[0] // 3, weight, first_out, last_out, flat, wide)


def cand_body(weight, head, first_out, last_out, head_out, flat, wide, eights):
    width = head.shape[2]
    lay_out(width, weight, first_out, last_out, flat, wide)
    eights[...] = jnp.zeros_like(eights)
    for o in range(head.shape[0]):
        eights[pl.ds(o, 27, stride=8), :width] = head[o].astype(F32)
    head_out[...] = eights[:, :width].astype(BF16)


def held_rows(part, planes, rows):
    def held(j):
        if 3 <= j < 3 + rows:
            return {"own": [(3, 3 + planes)], "face": [(0, 3), (3 + planes, 6 + planes)], "corner": []}[part]
        return {"own": [], "face": [(3, 3 + planes)], "corner": [(0, 3), (3 + planes, 6 + planes)]}[part]

    return held


def slots_of(part, planes, rows):
    slots = {}
    held = held_rows(part, planes, rows)
    for z in range(planes):
        for j in range(rows + 6):
            for first, last in held(j):
                for plane in range(max(z, first), min(z + 7, last)):
                    for y in range(rows):
                        if 0 <= j - y <= 6:
                            slots[z, y, (plane - z) * 7 + j - y] = len(slots)
    return slots


def corr_part(part, planes_out, rows_out, tt, s_flat, pairs):
    channels = s_flat.shape[1]
    sub = lax.broadcasted_iota(jnp.int32, (8, LANES), 0)
    cell = lax.broadcasted_iota(jnp.int32, (8, LANES), 1)
    block_of = (cell + 4 - sub + 8) // 8 - 1
    held, slots = held_rows(part, planes_out, rows_out), slots_of(part, planes_out, rows_out)

    for z in range(planes_out):
        for j in range(rows_out + 6):
            ys = [y for y in range(rows_out) if 0 <= j - y <= 6]
            lo, hi = ys[0] * LANES, (ys[-1] + 1) * LANES
            for first, last in held(j):
                first, last = max(z, first), min(z + 7, last)
                if first >= last:
                    continue
                lhs = tt[j, first:last].reshape((last - first) * LANES, channels)
                prod = jnp.dot(lhs, s_flat[z, :, lo:hi], preferred_element_type=F32)
                for plane in range(first, last):
                    for n, y in enumerate(ys):
                        got = jnp.zeros((8, LANES), F32)
                        for k in range(LANES // 8):
                            at = (plane - first) * LANES + 8 * k
                            piece = prod[at : at + 8, n * LANES : (n + 1) * LANES]
                            got = jnp.where(block_of == k, piece, got)
                        pairs[slots[z, y, (plane - z) * 7 + j - y]] = got


def encode(planes, rows, scale, parts, wc):
    wide = rows * LANES
    found = {}
    for part, pairs in parts.items():
        found.update({key: (pairs, slot) for key, slot in slots_of(part, planes, rows).items()})
    turn = (3 - lax.broadcasted_iota(jnp.int32, (1, 8, LANES), 2)) & 7
    turn = jnp.concatenate([turn] * rows, axis=2)
    results = []
    for z in range(planes):
        made = []
        for pair in range(49):
            row = []
            for y in range(rows):
                pairs, slot = found[z, y, pair]
                row.append(pairs[slot])
            made.append(jnp.concatenate(row, axis=1)[None])
        got = jnp.concatenate(made, axis=0)
        for bit in (1, 2, 4):
            got = jnp.where((turn & bit) != 0, pltpu.roll(got, bit, 1), got)
        got = (got * scale).reshape(49 * 8, wide).astype(BF16)
        results.append(jnp.dot(wc[...], got, preferred_element_type=F32))
    return results


def put_block(tt, block, ok, row, plane):
    def store(value):
        for p in range(block.shape[0]):
            for y in range(block.shape[1]):
                tt[row + y, plane + p] = value(p, y)

    if ok is None:
        store(lambda p, y: block[p, y].T)
        return

    @pl.when(ok)
    def _():
        store(lambda p, y: block[p, y].T)

    @pl.when(jnp.logical_not(ok))
    def _():
        store(lambda p, y: jnp.zeros(tt.shape[2:], BF16))


def column(row):
    return jnp.broadcast_to(row, (LANES, row.shape[1])).T


def own_body(
    w_reset, w_update, source, own, w_corr, hidden, motion, w_motion, bias_encoder, bias_update, bias_reset, bias_cand, bias_head,
    pairs, wc, h_first, h_last, s_flat, hidden_here, motion_here, begun, small, re_old, re_new, update_here,
    tt, reset_here, flat, wide, arrived
):
    copies = [
        pltpu.make_async_copy(w_reset, reset_here, arrived.at[0]),
        pltpu.make_async_copy(w_update, update_here, arrived.at[1]),
    ]
    for copy in copies:
        copy.start()
    planes, rows = source.shape[:2]
    h_first[...] = hidden[:2]
    h_last[...] = hidden[planes - 2 :]
    hidden_here[...] = hidden[...]
    motion_here[...] = motion[...]
    width, outs = hidden.shape[2], motion.shape[2]
    for n, row in enumerate((bias_encoder, bias_update, bias_reset, bias_cand)):
        small[n : n + 1, :width] = row[...]
    for n in range(w_motion.shape[0]):
        small[4 + n : 5 + n, :width] = w_motion[n : n + 1, :]
    shift = column(bias_head[...])
    for z in range(planes):
        for y in range(rows):
            s_flat[z, :, y * LANES : (y + 1) * LANES] = source[z, y]
            begun[z, y] = jnp.zeros(begun.shape[2:], F32)
            begun[z, y, :outs] = motion[z, y] + shift
    at = lax.broadcasted_iota(jnp.int32, (w_corr.shape[1], 49 * 8), 0)
    to = lax.broadcasted_iota(jnp.int32, (w_corr.shape[1], 49 * 8), 1)
    pick = ((to & 7) < 7) & (at == (to >> 3) * 7 + (to & 7))
    wc[...] = jnp.dot(w_corr[...], jnp.where(pick, 1.0, 0.0).astype(BF16), preferred_element_type=F32).astype(BF16)
    put_block(tt, own, None, 3, 3)
    corr_part("own", planes, rows, tt, s_flat, pairs)
    copies[0].wait()
    lay_out(width, reset_here, re_old, re_new, flat, wide)
    copies[1].wait()


def corr_face_body(place, s_flat, low, high, mate, other, pairs, tt):
    planes, rows = s_flat.shape[0], s_flat.shape[2] // LANES
    odd = place[3]
    put_block(tt, low, place[0] == 1, 3, 0)
    put_block(tt, high, place[1] == 1, 3, 3 + planes)
    put_block(tt, mate, None, (3 + rows) * (1 - odd), 3)
    put_block(tt, other, place[2] == 1, (3 + rows) * odd, 3)

    corr_part("face", planes, rows, tt, s_flat, pairs)


def corr_corner_body(
    place, s_flat, motion, small, own_pairs, face_pairs, low_mate, low_other, high_mate, high_other, wc,
    enc, enc_first, enc_last, tt, pairs
):
    planes, rows, outs = motion.shape[:3]
    width = enc.shape[2]
    odd = place[3]
    mate_at, other_at = (3 + rows) * (1 - odd), (3 + rows) * odd
    put_block(tt, low_mate, place[0] == 1, mate_at, 0)
    put_block(tt, low_other, place[0] + place[2] == 2, other_at, 0)
    put_block(tt, high_mate, place[1] == 1, mate_at, 3 + planes)
    put_block(tt, high_other, place[1] + place[2] == 2, other_at, 3 + planes)
    shift = column(small[0:1, :width])
    moves = [column(small[4 + k : 5 + k, :width]) for k in range(outs)]
    corr_part("corner", planes, rows, tt, s_flat, pairs)
    scale = s_flat.shape[1] ** (-0.5)
    parts = {"own": own_pairs, "face": face_pairs, "corner": pairs}
    for z, got in enumerate(encode(planes, rows, scale, parts, wc)):
        for y in range(rows):
            total = got[:, y * LANES : (y + 1) * LANES]
            for k, move in enumerate(moves):
                total = total + move * motion[z, y, k : k + 1, :]
            value = jnp.maximum(total + shift, 0.0).astype(BF16)
            enc[z, y] = value
            if z < 2:
                enc_first[z, y] = value
            if z >= planes - 2:
                enc_last[z - planes + 2, y] = value


def pack_body(place, own, low, high, to_mate, to_other):
    width = to_mate.shape[1]
    planes, rows = own.shape[:2]
    odd = place[3]
    for y in range(width):
        mate_at, other_at = (rows - width) * (1 - odd) + y, (rows - width) * odd + y
        first = 0
        for block in (low, own, high):
            to_mate[first : first + block.shape[0], y] = block[:, mate_at]
            to_other[first : first + block.shape[0], y] = block[:, other_at]
            first += block.shape[0]


def rows_of(place, low, own, high, width, name, from_hbm=()):
    planes = low.shape[0] + own.shape[0] + high.shape[0]
    out = jax.ShapeDtypeStruct((planes, width) + own.shape[2:], own.dtype)
    return call(pack_body, (out, out), [], (own, low, high), name, 6, place, from_hbm)


def taps(field, z, row, rows):
    wide = rows * LANES
    got = []
    for a in range(3):
        for b in range(3):
            got.append(field[z + a, :, (row + b) * LANES : (row + b) * LANES + wide])
    return got + [jnp.zeros((32, wide), BF16)]


def conv(weight, rhs, rows):
    three = jnp.dot(weight, jnp.concatenate(rhs, axis=0), preferred_element_type=F32)
    width = three.shape[0] // 3
    cell = lax.broadcasted_iota(jnp.int32, (width, LANES), 1)
    out = []
    for y in range(rows):
        at = slice(y * LANES, (y + 1) * LANES)
        before = jnp.where(cell == 0, 0.0, pltpu.roll(three[:width, at], 1, 1))
        after = jnp.where(cell == LANES - 1, 0.0, pltpu.roll(three[2 * width :, at], LANES - 1, 1))
        out.append(three[width : 2 * width, at] + before + after)
    return out


def fill(place, field, own, z0, z1, mate, other):
    planes, rows, width = own.shape[:3]
    odd = place[3]

    def store(plane, y, value):
        at = y * LANES if isinstance(y, int) else pl.multiple_of(y * LANES, LANES)
        field[plane, :, pl.ds(at, LANES)] = value

    def store_if(ok, plane, y, value):
        @pl.when(ok)
        def _():
            store(plane, y, value())

        @pl.when(jnp.logical_not(ok))
        def _():
            store(plane, y, jnp.zeros((width, LANES), BF16))

    for plane in range(planes + 4):
        in_z = None
        if plane < 2:
            in_z = place[0]
        elif plane >= planes + 2:
            in_z = place[1]
        for y in range(rows):
            if plane < 2:
                store_if(in_z == 1, plane, y + 2, lambda: z0[plane, y])
            elif plane >= planes + 2:
                store_if(in_z == 1, plane, y + 2, lambda: z1[plane - planes - 2, y])
            else:
                store(plane, y + 2, own[plane - 2, y])
        for y in range(2):
            mate_at, other_at = y + (rows + 2) * (1 - odd), y + (rows + 2) * odd
            if in_z is None:
                store(plane, mate_at, mate[plane, y])
                store_if(place[2] == 1, plane, other_at, lambda: other[plane, y])
            else:
                store_if(in_z == 1, plane, mate_at, lambda: mate[plane, y])
                store_if(in_z + place[2] == 2, plane, other_at, lambda: other[plane, y])


def old_body(place, hidden, small, hz0, hz1, h_mate, h_other, a_up, a_re, update_out, reset_out, near_out, field):
    planes, rows = hidden.shape[:2]
    fill(place, field, hidden, hz0, hz1, h_mate, h_other)
    width = hidden.shape[2]
    up_shift, re_shift = column(small[1:2, :width]), column(small[2:3, :width])

    def reset_plane(z, carry):
        near_out[z] = field[z + 1, :, LANES : (rows + 3) * LANES]
        for y, got in enumerate(conv(a_re[...], taps(field, z, 0, rows + 2), rows + 2)):
            reset_out[z, y] = got + re_shift
        return carry

    lax.fori_loop(0, planes + 2, reset_plane, 0, unroll=True)

    def update_plane(z, carry):
        for y, got in enumerate(conv(a_up[...], taps(field, z + 1, 1, rows), rows)):
            update_out[z, y] = got + up_shift
        return carry

    lax.fori_loop(0, planes, update_plane, 0, unroll=True)


def gru_body(
    place, begun, small, near, update_old, reset_old, enc, ez0, ez1, e_mate, e_other, a_up, a_re, a_ca_old, a_ca_new,
    head, state_out, part_low, part_out, part_high, field, gated, state
):
    planes, rows, width = enc.shape[:3]
    fill(place, field, enc, ez0, ez1, e_mate, e_other)
    ca_shift = column(small[3:4, :width])

    def reset_plane(z, carry):
        for y, got in enumerate(conv(a_re[...], taps(field, z, 0, rows + 2), rows + 2)):
            at = slice(y * LANES, (y + 1) * LANES)
            gate = jax.nn.sigmoid(got + reset_old[z, y])
            gated[z, :, at] = (gate * near[z, :, at].astype(F32)).astype(BF16)
        return carry

    lax.fori_loop(0, planes + 2, reset_plane, 0, unroll=True)

    def state_plane(z, carry):
        new_taps = taps(field, z + 1, 1, rows)
        update = conv(a_up[...], new_taps, rows)
        both = jnp.concatenate([a_ca_old[...], a_ca_new[...]], axis=1)
        cand = conv(both, taps(gated, z, 0, rows) + new_taps, rows)
        for y in range(rows):
            gate = jax.nn.sigmoid(update[y] + update_old[z, y])
            new = jnp.tanh(cand[y] + ca_shift)
            old = near[z + 1, :, (y + 1) * LANES : (y + 2) * LANES].astype(F32)
            got = ((1.0 - gate) * old + gate * new).astype(BF16)
            state_out[z, y] = got
            state[z, :, y * LANES : (y + 1) * LANES] = got
        return carry

    lax.fori_loop(0, planes, state_plane, 0, unroll=True)

    cell = lax.broadcasted_iota(jnp.int32, (8, LANES), 1)
    sums = {}
    for z in range(planes):
        prod = jnp.dot(head[...], state[z], preferred_element_type=F32)
        for y in range(rows):
            for a in range(3):
                for b in range(3):
                    key = (z + 2 - a, y + 2 - b)
                    for c in range(3):
                        t = a * 9 + b * 3 + c
                        piece = prod[t * 8 : t * 8 + 8, y * LANES : (y + 1) * LANES]
                        slot = sums.setdefault(key, [None] * 3)
                        slot[c] = piece if slot[c] is None else slot[c] + piece
    for (z, y), (before, same, after) in sums.items():
        before = jnp.where(cell == 0, 0.0, pltpu.roll(before, 1, 1))
        after = jnp.where(cell == LANES - 1, 0.0, pltpu.roll(after, LANES - 1, 1))
        total = same + before + after
        if z == 0:
            part_low[0, y] = total
        elif z == planes + 1:
            part_high[0, y] = total
        elif 0 < y <= rows:
            part_out[z - 1, y] = total + begun[z - 1, y - 1]
        else:
            part_out[z - 1, y] = total


def mix_body(place, part, low, high, mine, to_mate, to_other):
    planes, rows = mine.shape[:2]
    odd = place[3]
    mate_at, other_at = (rows + 1) * (1 - odd), (rows + 1) * odd

    def added(z, at):
        total = part[z, at]
        if z == 0:
            total = total + jnp.where(place[0] == 1, low[0, at], 0.0)
        if z == planes - 1:
            total = total + jnp.where(place[1] == 1, high[0, at], 0.0)
        return total

    for z in range(planes):
        for y in range(rows):
            mine[z, y] = added(z, y + 1)
        to_mate[z, 0] = added(z, mate_at)
        to_other[z, 0] = added(z, other_at)


def last_body(place, mine, mate, other, out):
    planes, rows, outs = out.shape[:3]
    odd = place[3]
    for z in range(planes):
        for y in range(rows):
            out[z, y] = mine[z, y, :outs]
        mate_at, other_at = (rows - 1) * (1 - odd), (rows - 1) * odd
        out[z, mate_at] = out[z, mate_at] + mate[z, 0, :outs]

        @pl.when(place[2] == 1)
        def _():
            out[z, other_at] = out[z, other_at] + other[z, 0, :outs]


def on_device(
    source, target, hidden, motion, w_corr, w_motion, bias_encoder, w_update, bias_update,
    w_reset, bias_reset, w_cand, bias_cand, w_head, bias_head
):
    planes, rows, channels, cells = source.shape
    width = hidden.shape[2]
    wide = rows * LANES
    place = inside()

    t_low, t_high = planes_around(target[:3], target[-3:])
    t_mate, t_other = rows_around(*edges(target, 3))

    target_rows = pltpu.VMEM((rows + 6, planes + 6, LANES, channels), BF16)
    made = jax.ShapeDtypeStruct
    pairs = {part: made((len(slots_of(part, planes, rows)), 8, cells), F32) for part in ("own", "face", "corner")}
    two = made((2, rows, width, cells), BF16)
    eight = made((planes, rows, 8, cells), F32)
    laid = pltpu.HBM((3 * width, 7 * LANES), BF16)
    biases = [b[None, :] for b in (bias_encoder, bias_update, bias_reset, bias_cand, bias_head)]
    own, wc, h_first, h_last, s_flat, hidden_here, motion_here, begun, small, re_old, re_new, update_here = call(
        own_body,
        (pairs["own"], made((width, 49 * 8), BF16), two, two, made((planes, channels, wide), BF16))
        + (made(hidden.shape, BF16), made(motion.shape, F32), eight, made((8, LANES), F32), laid, laid)
        + (made(w_update.shape, BF16),),
        [target_rows, pltpu.VMEM(w_reset.shape, BF16)] + lay_out_scratch(width) + [pltpu.SemaphoreType.DMA((2,))],
        [w_reset, w_update, source, target, w_corr, hidden, motion, w_motion.T] + biases,
        "own",
        14,
        from_hbm=(pltpu.HBM,) * 2 + (pltpu.VMEM,) * 11,
    )
    t_low, own = lax.optimization_barrier((t_low, own))
    t_low_mate, t_low_other = rows_around(*edges(t_low, 3))
    update_here, t_low = lax.optimization_barrier((update_here, t_low))
    up_old, up_new = call(
        update_body, (laid, laid), lay_out_scratch(width), (update_here,), "lay_out_update", 8
    )
    t_high, up_new = lax.optimization_barrier((t_high, up_new))
    t_high_mate, t_high_other = rows_around(*edges(t_high, 3))
    h_first, h_last, t_low, t_high = lax.optimization_barrier((h_first, h_last, t_low, t_high))
    h_low, h_high = planes_around(h_first, h_last)
    face = call(
        corr_face_body, pairs["face"], [target_rows], (s_flat, t_low, t_high, t_mate, t_other), "face", 9, place
    )

    enc, enc_first, enc_last = call(
        corr_corner_body,
        (made(hidden.shape, BF16), two, two),
        [target_rows] + [pltpu.VMEM(pairs["corner"].shape, F32)],
        (s_flat, motion_here, small)
        + (own, face, t_low_mate, t_low_other, t_high_mate, t_high_other, wc),
        "corner",
        10,
        place,
    )
    e_low, e_high = planes_around(enc_first, enc_last)
    taps_head, enc = lax.optimization_barrier((jnp.transpose(w_head, (1, 0, 2)), enc))
    ca_old, ca_new, head = call(
        cand_body,
        (laid, laid, pltpu.HBM((27 * 8, width), BF16)),
        lay_out_scratch(width) + [pltpu.VMEM((27 * 8, LANES), F32)],
        (w_cand, taps_head),
        "lay_out_cand",
        8,
        from_hbm=(pltpu.VMEM,) * 2,
    )
    e_low, ca_new = lax.optimization_barrier((e_low, ca_new))
    h_low, h_high, enc = lax.optimization_barrier((h_low, h_high, enc))
    h_mate, h_other = rows_around(*rows_of(place, h_low, hidden_here, h_high, 2, "pack_hidden"))
    field = pltpu.VMEM((planes + 4, width, (rows + 4) * LANES), BF16)
    update_old, reset_old, near = call(
        old_body,
        (
            jax.ShapeDtypeStruct((planes, rows, width, cells), F32),
            jax.ShapeDtypeStruct((planes + 2, rows + 2, width, cells), F32),
            jax.ShapeDtypeStruct((planes + 2, width, (rows + 2) * LANES), BF16),
        ),
        [field],
        (hidden_here, small, h_low, h_high, h_mate, h_other, up_old, re_old),
        "old",
        10,
        place,
    )
    e_mate, e_other = rows_around(*rows_of(place, e_low, enc, e_high, 2, "pack_encoded"))

    ring = lambda n: jax.ShapeDtypeStruct((n, rows + 2, 8, cells), F32)
    state_out, part_low, part, part_high = call(
        gru_body,
        (jax.ShapeDtypeStruct((planes, rows, width, cells), BF16), ring(1), ring(planes), ring(1)),
        [
            field,
            pltpu.VMEM((planes + 2, width, (rows + 2) * LANES), BF16),
            pltpu.VMEM((planes, width, wide), BF16),
        ],
        (begun, small, near, update_old, reset_old, enc, e_low, e_high, e_mate, e_other)
        + (up_new, re_new, ca_old, ca_new, head),
        "gru",
        12,
        place,
        kept=False,
    )
    low, high = planes_around(part_low, part_high)
    row = jax.ShapeDtypeStruct((planes, 1, 8, cells), F32)
    mine, to_mate, to_other = call(
        mix_body,
        (jax.ShapeDtypeStruct((planes, rows, 8, cells), F32), row, row),
        [],
        (part, low, high),
        "mix",
        4,
        place,
    )
    mate, other = rows_around(to_mate, to_other)
    motion_out = call(
        last_body,
        jax.ShapeDtypeStruct(motion.shape, F32),
        [],
        (mine, mate, other),
        "last",
        4,
        place,
        kept=False,
    )
    return state_out, motion_out


def solution(mesh):
    split = P("gz", "gy", None, None)
    return jax.shard_map(
        on_device,
        mesh=mesh,
        in_specs=(split,) * 4 + (P(),) * 11,
        out_specs=(split, split),
        check_vma=False,
    )
```

```python
import functools

import jax
import jax.numpy as jnp
from jax import lax
from jax.experimental import pallas as pl
from jax.experimental.pallas import tpu as pltpu
from jax.sharding import PartitionSpec as P

F32 = jnp.float32
BF16 = jnp.bfloat16
LANES = 128
MIB = 1024 * 1024


def around(block, axis, step):
    count = lax.axis_size(axis)
    return lax.ppermute(block, axis, [(i, (i + step) % count) for i in range(count)])


def planes_around(first, last):
    return around(last, "gz", 1), around(first, "gz", -1)


def rows_of_mate(to_mate):
    count = lax.axis_size("gy")
    return lax.ppermute(to_mate, "gy", [(i, i ^ 1) for i in range(count)])


def rows_of_other(to_other):
    count = lax.axis_size("gy")
    return lax.ppermute(to_other, "gy", [(i, ((i + 1) ^ 1) - 1) for i in range(1, count - 1)])


def rows_around(to_mate, to_other):
    other = rows_of_other(to_other)
    return rows_of_mate(to_mate), other


def edges(block, width):
    rows = block.shape[1]
    if rows == width:
        return block, block
    odd = lax.axis_index("gy") % 2
    to_mate = lax.dynamic_slice_in_dim(block, (rows - width) * (1 - odd), width, axis=1)
    return to_mate, lax.dynamic_slice_in_dim(block, (rows - width) * odd, width, axis=1)


def inside():
    z, y = lax.axis_index("gz"), lax.axis_index("gy")
    odd = y % 2
    end = jnp.where(odd == 1, lax.axis_size("gy") - 1, 0)
    return jnp.stack([z > 0, z < lax.axis_size("gz") - 1, y != end, odd == 1]).astype(jnp.int32)


def vmem(count):
    return [pl.BlockSpec(memory_space=pltpu.VMEM)] * count


def call(body, out_shape, scratch, args, name, mib, place=None, from_hbm=(), kept=True):
    struct = lambda o: isinstance(o, jax.ShapeDtypeStruct)
    in_specs = vmem(len(args))
    for n, given in enumerate(from_hbm):
        in_specs[n] = pl.BlockSpec(memory_space=given)
    args = [pltpu.with_memory_space_constraint(a, pltpu.HBM if n < len(from_hbm) else pltpu.VMEM) for n, a in enumerate(args)]
    if place is not None:
        args = [place] + args
        in_specs = [pl.BlockSpec(memory_space=pltpu.SMEM)] + in_specs
    return pl.pallas_call(
        body,
        out_shape=jax.tree.map(lambda o: pltpu.VMEM(o.shape, o.dtype) if kept and struct(o) else o, out_shape),
        in_specs=in_specs,
        out_specs=jax.tree.map(lambda _: pl.BlockSpec(memory_space=pltpu.VMEM), out_shape),
        scratch_shapes=scratch,
        compiler_params=pltpu.CompilerParams(vmem_limit_bytes=mib * MIB),
        cost_estimate=pl.CostEstimate(flops=1000, bytes_accessed=1000, transcendentals=0),
        name=name,
    )(*args)


def lay_out(width, weight, first_out, last_out, flat, wide):
    pieces = width * 2 * width // LANES
    pitch = pieces + 1
    half = width // 2
    lane = lax.broadcasted_iota(jnp.int32, (half, LANES), 1)

    def turn(value, by):
        return pltpu.roll(value, by, 1)

    def packed(parts):
        made = []
        for first in range(0, 9, 4):
            group = parts[first : first + 4]
            if len(group) == 1:
                made.append(jnp.where(lane < 96, group[0], 0.0))
                continue
            one, two = turn(group[1], 96), turn(group[2], 64)
            made.append(jnp.where(lane < 96, group[0], one))
            made.append(jnp.where(lane < 64, one, two))
            made.append(jnp.where(lane < 32, two, turn(group[3], 32)))
        return made

    def spread(j, carry):
        got = weight[:, pl.ds(pl.multiple_of(j * LANES, LANES), LANES)].astype(F32)
        for first in range(0, 27, 8):
            size = min(8, 27 - first)
            flat[pl.ds(j + first * pitch, size, stride=pitch), :] = got[first : first + size]
        return carry

    lax.fori_loop(0, pieces, spread, 0, unroll=8)

    for c in range(3):
        rows = [[], [], [], []]
        for ab in range(9):
            first, mid, last = [flat[pl.ds((ab * 3 + c) * pitch + k, half, stride=3), :] for k in range(3)]
            rows[0].append(first)
            rows[1].append(turn(jnp.where(lane < 64, last, mid), 64))
            rows[2].append(turn(jnp.where(lane >= 96, first, mid), 32))
            rows[3].append(turn(last, 96))
        for part in range(4):
            for k, chunk in enumerate(packed(rows[part])):
                wide[part // 2, k, pl.ds(c * width + part % 2, half, stride=2), :] = chunk
    for part, out in enumerate((first_out, last_out)):
        for chunk in range(7):
            out[:, chunk * LANES : (chunk + 1) * LANES] = wide[part, chunk].astype(BF16)


def lay_out_scratch(width):
    pitch = width * 2 * width // LANES + 1
    return [pltpu.VMEM((27 * pitch, LANES), F32), pltpu.VMEM((2, 7, 3 * width, LANES), F32)]


def update_body(weight, first_out, last_out, flat, wide):
    lay_out(first_out.shape[0] // 3, weight, first_out, last_out, flat, wide)


def cand_body(weight, head, first_out, last_out, head_out, flat, wide, eights):
    width = head.shape[2]
    lay_out(width, weight, first_out, last_out, flat, wide)
    eights[...] = jnp.zeros_like(eights)
    for o in range(head.shape[0]):
        eights[pl.ds(o, 27, stride=8), :width] = head[o].astype(F32)
    head_out[...] = eights[:, :width].astype(BF16)


def held_rows(part, planes, rows):
    def held(j):
        if 3 <= j < 3 + rows:
            return {"own": [(3, 3 + planes)], "face": [(0, 3), (3 + planes, 6 + planes)], "corner": []}[part]
        return {"own": [], "face": [(3, 3 + planes)], "corner": [(0, 3), (3 + planes, 6 + planes)]}[part]

    return held


def slots_of(part, planes, rows):
    slots = {}
    held = held_rows(part, planes, rows)
    for z in range(planes):
        for j in range(rows + 6):
            for first, last in held(j):
                for plane in range(max(z, first), min(z + 7, last)):
                    for y in range(rows):
                        if 0 <= j - y <= 6:
                            slots[z, y, (plane - z) * 7 + j - y] = len(slots)
    return slots


def corr_part(part, planes_out, rows_out, tt, s_flat, pairs):
    channels = s_flat.shape[1]
    sub = lax.broadcasted_iota(jnp.int32, (8, LANES), 0)
    cell = lax.broadcasted_iota(jnp.int32, (8, LANES), 1)
    block_of = (cell + 4 - sub + 8) // 8 - 1
    held, slots = held_rows(part, planes_out, rows_out), slots_of(part, planes_out, rows_out)

    for z in range(planes_out):
        for j in range(rows_out + 6):
            ys = [y for y in range(rows_out) if 0 <= j - y <= 6]
            lo, hi = ys[0] * LANES, (ys[-1] + 1) * LANES
            for first, last in held(j):
                first, last = max(z, first), min(z + 7, last)
                if first >= last:
                    continue
                lhs = tt[j, first:last].reshape((last - first) * LANES, channels)
                prod = jnp.dot(lhs, s_flat[z, :, lo:hi], preferred_element_type=F32)
                for plane in range(first, last):
                    for n, y in enumerate(ys):
                        got = jnp.zeros((8, LANES), F32)
                        for k in range(LANES // 8):
                            at = (plane - first) * LANES + 8 * k
                            piece = prod[at : at + 8, n * LANES : (n + 1) * LANES]
                            got = jnp.where(block_of == k, piece, got)
                        pairs[slots[z, y, (plane - z) * 7 + j - y]] = got


def encode(planes, rows, scale, parts, wc):
    wide = rows * LANES
    found = {}
    for part, pairs in parts.items():
        found.update({key: (pairs, slot) for key, slot in slots_of(part, planes, rows).items()})
    turn = (3 - lax.broadcasted_iota(jnp.int32, (1, 8, LANES), 2)) & 7
    turn = jnp.concatenate([turn] * rows, axis=2)
    results = []
    for z in range(planes):
        made = []
        for pair in range(49):
            row = []
            for y in range(rows):
                pairs, slot = found[z, y, pair]
                row.append(pairs[slot])
            made.append(jnp.concatenate(row, axis=1)[None])
        got = jnp.concatenate(made, axis=0)
        for bit in (1, 2, 4):
            got = jnp.where((turn & bit) != 0, pltpu.roll(got, bit, 1), got)
        got = (got * scale).reshape(49 * 8, wide).astype(BF16)
        results.append(jnp.dot(wc[...], got, preferred_element_type=F32))
    return results


def put_block(tt, block, ok, row, plane):
    def store(value):
        for p in range(block.shape[0]):
            for y in range(block.shape[1]):
                tt[row + y, plane + p] = value(p, y)

    if ok is None:
        store(lambda p, y: block[p, y].T)
        return

    @pl.when(ok)
    def _():
        store(lambda p, y: block[p, y].T)

    @pl.when(jnp.logical_not(ok))
    def _():
        store(lambda p, y: jnp.zeros(tt.shape[2:], BF16))


def column(row):
    return jnp.broadcast_to(row, (LANES, row.shape[1])).T


def own_body(
    w_reset, w_update, source, own, w_corr, hidden, motion, w_motion, bias_encoder, bias_update, bias_reset, bias_cand, bias_head,
    pairs, wc, h_first, h_last, s_flat, hidden_here, motion_here, begun, small, re_old, re_new, update_here,
    tt, reset_here, flat, wide, arrived
):
    copies = [
        pltpu.make_async_copy(w_reset, reset_here, arrived.at[0]),
        pltpu.make_async_copy(w_update, update_here, arrived.at[1]),
    ]
    for copy in copies:
        copy.start()
    planes, rows = source.shape[:2]
    h_first[...] = hidden[:2]
    h_last[...] = hidden[planes - 2 :]
    hidden_here[...] = hidden[...]
    motion_here[...] = motion[...]
    width, outs = hidden.shape[2], motion.shape[2]
    for n, row in enumerate((bias_encoder, bias_update, bias_reset, bias_cand)):
        small[n : n + 1, :width] = row[...]
    for n in range(w_motion.shape[0]):
        small[4 + n : 5 + n, :width] = w_motion[n : n + 1, :]
    shift = column(bias_head[...])
    for z in range(planes):
        for y in range(rows):
            s_flat[z, :, y * LANES : (y + 1) * LANES] = source[z, y]
            begun[z, y] = jnp.zeros(begun.shape[2:], F32)
            begun[z, y, :outs] = motion[z, y] + shift
    at = lax.broadcasted_iota(jnp.int32, (w_corr.shape[1], 49 * 8), 0)
    to = lax.broadcasted_iota(jnp.int32, (w_corr.shape[1], 49 * 8), 1)
    pick = ((to & 7) < 7) & (at == (to >> 3) * 7 + (to & 7))
    wc[...] = jnp.dot(w_corr[...], jnp.where(pick, 1.0, 0.0).astype(BF16), preferred_element_type=F32).astype(BF16)
    put_block(tt, own, None, 3, 3)
    corr_part("own", planes, rows, tt, s_flat, pairs)
    copies[0].wait()
    lay_out(width, reset_here, re_old, re_new, flat, wide)
    copies[1].wait()


def corr_face_body(place, s_flat, low, high, mate, other, pairs, tt):
    planes, rows = s_flat.shape[0], s_flat.shape[2] // LANES
    odd = place[3]
    put_block(tt, low, place[0] == 1, 3, 0)
    put_block(tt, high, place[1] == 1, 3, 3 + planes)
    put_block(tt, mate, None, (3 + rows) * (1 - odd), 3)
    put_block(tt, other, place[2] == 1, (3 + rows) * odd, 3)

    corr_part("face", planes, rows, tt, s_flat, pairs)


def corr_corner_body(
    place, s_flat, motion, small, own_pairs, face_pairs, low_mate, low_other, high_mate, high_other, wc,
    enc, enc_first, enc_last, tt, pairs
):
    planes, rows, outs = motion.shape[:3]
    width = enc.shape[2]
    odd = place[3]
    mate_at, other_at = (3 + rows) * (1 - odd), (3 + rows) * odd
    put_block(tt, low_mate, place[0] == 1, mate_at, 0)
    put_block(tt, low_other, place[0] + place[2] == 2, other_at, 0)
    put_block(tt, high_mate, place[1] == 1, mate_at, 3 + planes)
    put_block(tt, high_other, place[1] + place[2] == 2, other_at, 3 + planes)
    shift = column(small[0:1, :width])
    moves = [column(small[4 + k : 5 + k, :width]) for k in range(outs)]
    corr_part("corner", planes, rows, tt, s_flat, pairs)
    scale = s_flat.shape[1] ** (-0.5)
    parts = {"own": own_pairs, "face": face_pairs, "corner": pairs}
    for z, got in enumerate(encode(planes, rows, scale, parts, wc)):
        for y in range(rows):
            total = got[:, y * LANES : (y + 1) * LANES]
            for k, move in enumerate(moves):
                total = total + move * motion[z, y, k : k + 1, :]
            value = jnp.maximum(total + shift, 0.0).astype(BF16)
            enc[z, y] = value
            if z < 2:
                enc_first[z, y] = value
            if z >= planes - 2:
                enc_last[z - planes + 2, y] = value


def pack_body(place, own, low, high, to_mate, to_other):
    width = to_mate.shape[1]
    planes, rows = own.shape[:2]
    odd = place[3]
    for y in range(width):
        mate_at, other_at = (rows - width) * (1 - odd) + y, (rows - width) * odd + y
        first = 0
        for block in (low, own, high):
            to_mate[first : first + block.shape[0], y] = block[:, mate_at]
            to_other[first : first + block.shape[0], y] = block[:, other_at]
            first += block.shape[0]


def rows_of(place, low, own, high, width, name, from_hbm=()):
    planes = low.shape[0] + own.shape[0] + high.shape[0]
    out = jax.ShapeDtypeStruct((planes, width) + own.shape[2:], own.dtype)
    return call(pack_body, (out, out), [], (own, low, high), name, 6, place, from_hbm)


def taps(field, z, row, rows):
    wide = rows * LANES
    got = []
    for a in range(3):
        for b in range(3):
            got.append(field[z + a, :, (row + b) * LANES : (row + b) * LANES + wide])
    return got + [jnp.zeros((32, wide), BF16)]


def side_by_side(field, planes, row, rows):
    return [jnp.concatenate(parts, axis=1) for parts in zip(*[taps(field, z, row, rows) for z in planes])]


def conv(weight, rhs, rows):
    three = jnp.dot(weight, jnp.concatenate(rhs, axis=0), preferred_element_type=F32)
    width = three.shape[0] // 3
    cell = lax.broadcasted_iota(jnp.int32, (width, LANES), 1)
    out = []
    for y in range(rows):
        at = slice(y * LANES, (y + 1) * LANES)
        before = jnp.where(cell == 0, 0.0, pltpu.roll(three[:width, at], 1, 1))
        after = jnp.where(cell == LANES - 1, 0.0, pltpu.roll(three[2 * width :, at], LANES - 1, 1))
        out.append(three[width : 2 * width, at] + before + after)
    return out


def fill(place, field, own, z0, z1, mate, other):
    planes, rows, width = own.shape[:3]
    odd = place[3]

    def store(plane, y, value):
        at = y * LANES if isinstance(y, int) else pl.multiple_of(y * LANES, LANES)
        field[plane, :, pl.ds(at, LANES)] = value

    def store_if(ok, plane, y, value):
        @pl.when(ok)
        def _():
            store(plane, y, value())

        @pl.when(jnp.logical_not(ok))
        def _():
            store(plane, y, jnp.zeros((width, LANES), BF16))

    for plane in range(planes + 4):
        in_z = None
        if plane < 2:
            in_z = place[0]
        elif plane >= planes + 2:
            in_z = place[1]
        for y in range(rows):
            if plane < 2:
                store_if(in_z == 1, plane, y + 2, lambda: z0[plane, y])
            elif plane >= planes + 2:
                store_if(in_z == 1, plane, y + 2, lambda: z1[plane - planes - 2, y])
            else:
                store(plane, y + 2, own[plane - 2, y])
        for y in range(2):
            mate_at, other_at = y + (rows + 2) * (1 - odd), y + (rows + 2) * odd
            if in_z is None:
                store(plane, mate_at, mate[plane, y])
                store_if(place[2] == 1, plane, other_at, lambda: other[plane, y])
            else:
                store_if(in_z == 1, plane, mate_at, lambda: mate[plane, y])
                store_if(in_z + place[2] == 2, plane, other_at, lambda: other[plane, y])


def old_body(place, hidden, small, hz0, hz1, h_mate, h_other, a_up, a_re, update_out, reset_out, near_out, field):
    planes, rows = hidden.shape[:2]
    fill(place, field, hidden, hz0, hz1, h_mate, h_other)
    width = hidden.shape[2]
    up_shift, re_shift = column(small[1:2, :width]), column(small[2:3, :width])

    for z in range(planes + 2):
        near_out[z] = field[z + 1, :, LANES : (rows + 3) * LANES]
    for n, got in enumerate(conv(a_re[...], side_by_side(field, range(planes + 2), 0, rows + 2), (planes + 2) * (rows + 2))):
        reset_out[n // (rows + 2), n % (rows + 2)] = got + re_shift
    for n, got in enumerate(conv(a_up[...], side_by_side(field, range(1, planes + 1), 1, rows), planes * rows)):
        update_out[n // rows, n % rows] = got + up_shift


def new_states(planes, rows, small, near, update_old, field, gated, a_up, a_ca_old, a_ca_new):
    width = near.shape[1]
    ca_shift = column(small[3:4, :width])
    new_taps = side_by_side(field, [z + 1 for z in planes], 1, rows)
    update = conv(a_up[...], new_taps, len(planes) * rows)
    both = jnp.concatenate([a_ca_old[...], a_ca_new[...]], axis=1)
    cand = conv(both, side_by_side(gated, planes, 0, rows) + new_taps, len(planes) * rows)
    for n in range(len(planes) * rows):
        z, y = planes[n // rows], n % rows
        gate = jax.nn.sigmoid(update[n] + update_old[z, y])
        new = jnp.tanh(cand[n] + ca_shift)
        old = near[z + 1, :, (y + 1) * LANES : (y + 2) * LANES].astype(F32)
        yield z, y, ((1.0 - gate) * old + gate * new).astype(BF16)


def head_parts(head, state, planes, rows):
    cell = lax.broadcasted_iota(jnp.int32, (8, LANES), 1)
    sums, parts = {}, {}
    for n, z in enumerate(planes):
        prod = jnp.dot(head[...], state[n], preferred_element_type=F32)
        for y in range(rows):
            for a in range(3):
                for b in range(3):
                    for c in range(3):
                        t = a * 9 + b * 3 + c
                        piece = prod[t * 8 : t * 8 + 8, y * LANES : (y + 1) * LANES]
                        slot = sums.setdefault((z + 2 - a, y + 2 - b), [None] * 3)
                        slot[c] = piece if slot[c] is None else slot[c] + piece
    for key, (before, same, after) in sums.items():
        before = jnp.where(cell == 0, 0.0, pltpu.roll(before, 1, 1))
        after = jnp.where(cell == LANES - 1, 0.0, pltpu.roll(after, LANES - 1, 1))
        parts[key] = same + before + after
    return parts


def outer_planes(planes):
    return sorted({0, planes - 1})


def gru_outer_body(
    place, begun, small, near, update_old, reset_old, enc, ez0, ez1, e_mate, e_other, a_up, a_re, a_ca_old, a_ca_new, head,
    part_low, part_out, part_high, field, gated, outer, state
):
    planes, rows = enc.shape[:2]
    fill(place, field, enc, ez0, ez1, e_mate, e_other)
    every = range(planes + 2)
    for n, got in enumerate(conv(a_re[...], side_by_side(field, every, 0, rows + 2), (planes + 2) * (rows + 2))):
        z, y = n // (rows + 2), n % (rows + 2)
        at = slice(y * LANES, (y + 1) * LANES)
        gate = jax.nn.sigmoid(got + reset_old[z, y])
        gated[z, :, at] = (gate * near[z, :, at].astype(F32)).astype(BF16)

    ends = outer_planes(planes)
    for z, y, got in new_states(ends, rows, small, near, update_old, field, gated, a_up, a_ca_old, a_ca_new):
        outer[ends.index(z), y] = got
        state[ends.index(z), :, y * LANES : (y + 1) * LANES] = got

    parts = head_parts(head, state, ends, rows)
    for z in range(planes + 2):
        for y in range(rows + 2):
            total = parts.get((z, y))
            if 0 < z <= planes and 0 < y <= rows:
                total = begun[z - 1, y - 1] if total is None else total + begun[z - 1, y - 1]
            if total is None:
                total = jnp.zeros(part_out.shape[2:], F32)
            if z == 0:
                part_low[0, y] = total
            elif z == planes + 1:
                part_high[0, y] = total
            else:
                part_out[z - 1, y] = total


def gru_inner_body(
    small, near, update_old, field, gated, a_up, a_ca_old, a_ca_new, head, part, outer, state_out, part_out, state
):
    planes, rows = state_out.shape[:2]
    ends = outer_planes(planes)
    inner = [z for z in range(planes) if z not in ends]
    for n, z in enumerate(ends):
        state_out[z] = outer[n]
    part_out[...] = part[...]
    for z, y, got in new_states(inner, rows, small, near, update_old, field, gated, a_up, a_ca_old, a_ca_new):
        state_out[z, y] = got
        state[inner.index(z), :, y * LANES : (y + 1) * LANES] = got
    for (z, y), total in head_parts(head, state, inner, rows).items():
        part_out[z - 1, y] = part[z - 1, y] + total


def mix_body(place, part, low, high, mine, to_mate, to_other):
    planes, rows = mine.shape[:2]
    odd = place[3]
    mate_at, other_at = (rows + 1) * (1 - odd), (rows + 1) * odd

    def added(z, at):
        total = part[z, at]
        if z == 0:
            total = total + jnp.where(place[0] == 1, low[0, at], 0.0)
        if z == planes - 1:
            total = total + jnp.where(place[1] == 1, high[0, at], 0.0)
        return total

    for z in range(planes):
        for y in range(rows):
            mine[z, y] = added(z, y + 1)
        to_mate[z, 0] = added(z, mate_at)
        to_other[z, 0] = added(z, other_at)


def on_device(
    source, target, hidden, motion, w_corr, w_motion, bias_encoder, w_update, bias_update,
    w_reset, bias_reset, w_cand, bias_cand, w_head, bias_head
):
    planes, rows, channels, cells = source.shape
    width = hidden.shape[2]
    wide = rows * LANES
    place = inside()

    t_low, t_high = planes_around(target[:3], target[-3:])
    to_mate, to_other = edges(target, 3)
    t_other = rows_of_other(to_other)

    target_rows = pltpu.VMEM((rows + 6, planes + 6, LANES, channels), BF16)
    made = jax.ShapeDtypeStruct
    pairs = {part: made((len(slots_of(part, planes, rows)), 8, cells), F32) for part in ("own", "face", "corner")}
    two = made((2, rows, width, cells), BF16)
    eight = made((planes, rows, 8, cells), F32)
    laid = pltpu.HBM((3 * width, 7 * LANES), BF16)
    biases = [b[None, :] for b in (bias_encoder, bias_update, bias_reset, bias_cand, bias_head)]
    own, wc, h_first, h_last, s_flat, hidden_here, motion_here, begun, small, re_old, re_new, update_here = call(
        own_body,
        (pairs["own"], made((width, 49 * 8), BF16), two, two, made((planes, channels, wide), BF16))
        + (made(hidden.shape, BF16), made(motion.shape, F32), eight, made((8, LANES), F32), laid, laid)
        + (made(w_update.shape, BF16),),
        [target_rows, pltpu.VMEM(w_reset.shape, BF16)] + lay_out_scratch(width) + [pltpu.SemaphoreType.DMA((2,))],
        [w_reset, w_update, source, target, w_corr, hidden, motion, w_motion.T] + biases,
        "own",
        14,
        from_hbm=(pltpu.HBM,) * 2 + (pltpu.VMEM,) * 11,
    )
    t_low, to_mate, own = lax.optimization_barrier((t_low, to_mate, own))
    t_mate = rows_of_mate(to_mate)
    t_low_mate, t_low_other = rows_around(*edges(t_low, 3))
    update_here, t_low = lax.optimization_barrier((update_here, t_low))
    up_old, up_new = call(
        update_body, (laid, laid), lay_out_scratch(width), (update_here,), "lay_out_update", 8
    )
    t_high, up_new = lax.optimization_barrier((t_high, up_new))
    t_high_mate, t_high_other = rows_around(*edges(t_high, 3))
    h_first, h_last, t_low, t_high = lax.optimization_barrier((h_first, h_last, t_low, t_high))
    h_low, h_high = planes_around(h_first, h_last)
    face = call(
        corr_face_body, pairs["face"], [target_rows], (s_flat, t_low, t_high, t_mate, t_other), "face", 9, place
    )

    enc, enc_first, enc_last = call(
        corr_corner_body,
        (made(hidden.shape, BF16), two, two),
        [target_rows] + [pltpu.VMEM(pairs["corner"].shape, F32)],
        (s_flat, motion_here, small)
        + (own, face, t_low_mate, t_low_other, t_high_mate, t_high_other, wc),
        "corner",
        10,
        place,
    )
    e_low, e_high = planes_around(enc_first, enc_last)
    taps_head, enc = lax.optimization_barrier((jnp.transpose(w_head, (1, 0, 2)), enc))
    ca_old, ca_new, head = call(
        cand_body,
        (laid, laid, pltpu.HBM((27 * 8, width), BF16)),
        lay_out_scratch(width) + [pltpu.VMEM((27 * 8, LANES), F32)],
        (w_cand, taps_head),
        "lay_out_cand",
        8,
        from_hbm=(pltpu.VMEM,) * 2,
    )
    e_low, ca_new = lax.optimization_barrier((e_low, ca_new))
    h_low, h_high, enc = lax.optimization_barrier((h_low, h_high, enc))
    h_mate, h_other = rows_around(*rows_of(place, h_low, hidden_here, h_high, 2, "pack_hidden"))
    field = pltpu.VMEM((planes + 4, width, (rows + 4) * LANES), BF16)
    update_old, reset_old, near = call(
        old_body,
        (
            jax.ShapeDtypeStruct((planes, rows, width, cells), F32),
            jax.ShapeDtypeStruct((planes + 2, rows + 2, width, cells), F32),
            jax.ShapeDtypeStruct((planes + 2, width, (rows + 2) * LANES), BF16),
        ),
        [field],
        (hidden_here, small, h_low, h_high, h_mate, h_other, up_old, re_old),
        "old",
        10,
        place,
    )
    e_mate, e_other = rows_around(*rows_of(place, e_low, enc, e_high, 2, "pack_encoded"))

    ring = lambda n: jax.ShapeDtypeStruct((n, rows + 2, 8, cells), F32)
    ends = len(outer_planes(planes))
    part_low, part, part_high, e_field, gated, outer = call(
        gru_outer_body,
        (ring(1), ring(planes), ring(1), made(field.shape, BF16))
        + (made((planes + 2, width, (rows + 2) * LANES), BF16), made((ends, rows, width, cells), BF16)),
        [pltpu.VMEM((ends, width, wide), BF16)],
        (begun, small, near, update_old, reset_old, enc, e_low, e_high, e_mate, e_other)
        + (up_new, re_new, ca_old, ca_new, head),
        "gru_outer",
        12,
        place,
    )
    low, high = planes_around(part_low, part_high)
    state_out, part = call(
        gru_inner_body,
        (pltpu.HBM(hidden.shape, BF16), ring(planes)),
        [pltpu.VMEM((planes - ends, width, wide), BF16)],
        (small, near, update_old, e_field, gated, up_new, ca_old, ca_new, head, part, outer),
        "gru_inner",
        12,
    )
    row = jax.ShapeDtypeStruct((planes, 1, 8, cells), F32)
    mine, to_mate, to_other = call(
        mix_body,
        (jax.ShapeDtypeStruct((planes, rows, 8, cells), F32), row, row),
        [],
        (part, low, high),
        "mix",
        4,
        place,
    )
    mate, other = rows_around(to_mate, to_other)
    other = jnp.where(place[2] == 1, other, 0.0)
    odd = place[3] == 1
    below, above = jnp.where(odd, mate, other), jnp.where(odd, other, mate)
    row = lax.broadcasted_iota(jnp.int32, mine.shape, 1)
    total = mine + jnp.where(row == 0, below, 0.0) + jnp.where(row == rows - 1, above, 0.0)
    motion_out = total[:, :, : motion.shape[2]]
    return state_out, motion_out


def solution(mesh):
    split = P("gz", "gy", None, None)
    return jax.shard_map(
        on_device,
        mesh=mesh,
        in_specs=(split,) * 4 + (P(),) * 11,
        out_specs=(split, split),
        check_vma=False,
    )
```

```python
import functools

import jax
import jax.numpy as jnp
from jax import lax
from jax.experimental import pallas as pl
from jax.experimental.pallas import tpu as pltpu
from jax.sharding import PartitionSpec as P

F32 = jnp.float32
BF16 = jnp.bfloat16
LANES = 128
MIB = 1024 * 1024


def around(block, axis, step):
    count = lax.axis_size(axis)
    return lax.ppermute(block, axis, [(i, (i + step) % count) for i in range(count)])


def planes_around(first, last):
    return around(last, "gz", 1), around(first, "gz", -1)


def rows_of_mate(to_mate):
    count = lax.axis_size("gy")
    return lax.ppermute(to_mate, "gy", [(i, i ^ 1) for i in range(count)])


def rows_of_other(to_other):
    count = lax.axis_size("gy")
    return lax.ppermute(to_other, "gy", [(i, ((i + 1) ^ 1) - 1) for i in range(1, count - 1)])


def rows_around(to_mate, to_other):
    other = rows_of_other(to_other)
    return rows_of_mate(to_mate), other


def edges(block, width):
    rows = block.shape[1]
    if rows == width:
        return block, block
    odd = lax.axis_index("gy") % 2
    to_mate = lax.dynamic_slice_in_dim(block, (rows - width) * (1 - odd), width, axis=1)
    return to_mate, lax.dynamic_slice_in_dim(block, (rows - width) * odd, width, axis=1)


def inside():
    z, y = lax.axis_index("gz"), lax.axis_index("gy")
    odd = y % 2
    end = jnp.where(odd == 1, lax.axis_size("gy") - 1, 0)
    return jnp.stack([z > 0, z < lax.axis_size("gz") - 1, y != end, odd == 1]).astype(jnp.int32)


def vmem(count):
    return [pl.BlockSpec(memory_space=pltpu.VMEM)] * count


def call(body, out_shape, scratch, args, name, mib, place=None, from_hbm=(), kept=True):
    struct = lambda o: isinstance(o, jax.ShapeDtypeStruct)
    in_specs = vmem(len(args))
    for n, given in enumerate(from_hbm):
        in_specs[n] = pl.BlockSpec(memory_space=given)
    args = [pltpu.with_memory_space_constraint(a, pltpu.HBM if n < len(from_hbm) else pltpu.VMEM) for n, a in enumerate(args)]
    if place is not None:
        args = [place] + args
        in_specs = [pl.BlockSpec(memory_space=pltpu.SMEM)] + in_specs
    return pl.pallas_call(
        body,
        out_shape=jax.tree.map(lambda o: pltpu.VMEM(o.shape, o.dtype) if kept and struct(o) else o, out_shape),
        in_specs=in_specs,
        out_specs=jax.tree.map(lambda _: pl.BlockSpec(memory_space=pltpu.VMEM), out_shape),
        scratch_shapes=scratch,
        compiler_params=pltpu.CompilerParams(vmem_limit_bytes=mib * MIB),
        cost_estimate=pl.CostEstimate(flops=1000, bytes_accessed=1000, transcendentals=0),
        name=name,
    )(*args)


def lay_out(width, weight, first_out, last_out, flat, wide):
    pieces = width * 2 * width // LANES
    pitch = pieces + 1
    half = width // 2
    lane = lax.broadcasted_iota(jnp.int32, (half, LANES), 1)

    def turn(value, by):
        return pltpu.roll(value, by, 1)

    def packed(parts):
        made = []
        for first in range(0, 9, 4):
            group = parts[first : first + 4]
            if len(group) == 1:
                made.append(jnp.where(lane < 96, group[0], 0.0))
                continue
            one, two = turn(group[1], 96), turn(group[2], 64)
            made.append(jnp.where(lane < 96, group[0], one))
            made.append(jnp.where(lane < 64, one, two))
            made.append(jnp.where(lane < 32, two, turn(group[3], 32)))
        return made

    def spread(j, carry):
        got = weight[:, pl.ds(pl.multiple_of(j * LANES, LANES), LANES)].astype(F32)
        for first in range(0, 27, 8):
            size = min(8, 27 - first)
            flat[pl.ds(j + first * pitch, size, stride=pitch), :] = got[first : first + size]
        return carry

    lax.fori_loop(0, pieces, spread, 0, unroll=8)

    for c in range(3):
        rows = [[], [], [], []]
        for ab in range(9):
            first, mid, last = [flat[pl.ds((ab * 3 + c) * pitch + k, half, stride=3), :] for k in range(3)]
            rows[0].append(first)
            rows[1].append(turn(jnp.where(lane < 64, last, mid), 64))
            rows[2].append(turn(jnp.where(lane >= 96, first, mid), 32))
            rows[3].append(turn(last, 96))
        for part in range(4):
            for k, chunk in enumerate(packed(rows[part])):
                wide[part // 2, k, pl.ds(c * width + part % 2, half, stride=2), :] = chunk
    for part, out in enumerate((first_out, last_out)):
        for chunk in range(7):
            out[:, chunk * LANES : (chunk + 1) * LANES] = wide[part, chunk].astype(BF16)


def lay_out_scratch(width):
    pitch = width * 2 * width // LANES + 1
    return [pltpu.VMEM((27 * pitch, LANES), F32), pltpu.VMEM((2, 7, 3 * width, LANES), F32)]


def update_body(weight, first_out, last_out, flat, wide):
    lay_out(first_out.shape[0] // 3, weight, first_out, last_out, flat, wide)


def cand_body(weight, head, first_out, last_out, head_out, flat, wide, eights):
    width = head.shape[2]
    lay_out(width, weight, first_out, last_out, flat, wide)
    eights[...] = jnp.zeros_like(eights)
    for o in range(head.shape[0]):
        eights[pl.ds(o, 27, stride=8), :width] = head[o].astype(F32)
    head_out[...] = eights[:, :width].astype(BF16)


def held_rows(part, planes, rows):
    def held(j):
        if 3 <= j < 3 + rows:
            return {"own": [(3, 3 + planes)], "face": [(0, 3), (3 + planes, 6 + planes)], "corner": []}[part]
        return {"own": [], "face": [(3, 3 + planes)], "corner": [(0, 3), (3 + planes, 6 + planes)]}[part]

    return held


def slots_of(part, planes, rows):
    slots = {}
    held = held_rows(part, planes, rows)
    for z in range(planes):
        for j in range(rows + 6):
            for first, last in held(j):
                for plane in range(max(z, first), min(z + 7, last)):
                    for y in range(rows):
                        if 0 <= j - y <= 6:
                            slots[z, y, (plane - z) * 7 + j - y] = len(slots)
    return slots


def corr_part(part, planes_out, rows_out, tt, s_flat, pairs):
    channels = s_flat.shape[1]
    sub = lax.broadcasted_iota(jnp.int32, (8, LANES), 0)
    cell = lax.broadcasted_iota(jnp.int32, (8, LANES), 1)
    block_of = (cell + 4 - sub + 8) // 8 - 1
    held, slots = held_rows(part, planes_out, rows_out), slots_of(part, planes_out, rows_out)

    for z in range(planes_out):
        for j in range(rows_out + 6):
            ys = [y for y in range(rows_out) if 0 <= j - y <= 6]
            lo, hi = ys[0] * LANES, (ys[-1] + 1) * LANES
            for first, last in held(j):
                first, last = max(z, first), min(z + 7, last)
                if first >= last:
                    continue
                lhs = tt[j, first:last].reshape((last - first) * LANES, channels)
                prod = jnp.dot(lhs, s_flat[z, :, lo:hi], preferred_element_type=F32)
                for plane in range(first, last):
                    for n, y in enumerate(ys):
                        got = jnp.zeros((8, LANES), F32)
                        for k in range(LANES // 8):
                            at = (plane - first) * LANES + 8 * k
                            piece = prod[at : at + 8, n * LANES : (n + 1) * LANES]
                            got = jnp.where(block_of == k, piece, got)
                        pairs[slots[z, y, (plane - z) * 7 + j - y]] = got


def encode(planes, rows, scale, parts, wc):
    wide = rows * LANES
    found = {}
    for part, pairs in parts.items():
        found.update({key: (pairs, slot) for key, slot in slots_of(part, planes, rows).items()})
    turn = (3 - lax.broadcasted_iota(jnp.int32, (1, 8, LANES), 2)) & 7
    turn = jnp.concatenate([turn] * rows, axis=2)
    columns = []
    for z in range(planes):
        made = []
        for pair in range(49):
            row = []
            for y in range(rows):
                pairs, slot = found[z, y, pair]
                row.append(pairs[slot])
            made.append(jnp.concatenate(row, axis=1)[None])
        got = jnp.concatenate(made, axis=0)
        for bit in (1, 2, 4):
            got = jnp.where((turn & bit) != 0, pltpu.roll(got, bit, 1), got)
        columns.append((got * scale).reshape(49 * 8, wide).astype(BF16))
    sums = jnp.dot(wc[...], jnp.concatenate(columns, axis=1), preferred_element_type=F32)
    return [sums[:, z * wide : (z + 1) * wide] for z in range(planes)]


def put_block(tt, block, ok, row, plane):
    def store(value):
        for p in range(block.shape[0]):
            for y in range(block.shape[1]):
                tt[row + y, plane + p] = value(p, y)

    if ok is None:
        store(lambda p, y: block[p, y].T)
        return

    @pl.when(ok)
    def _():
        store(lambda p, y: block[p, y].T)

    @pl.when(jnp.logical_not(ok))
    def _():
        store(lambda p, y: jnp.zeros(tt.shape[2:], BF16))


def column(row):
    return jnp.broadcast_to(row, (LANES, row.shape[1])).T


def own_body(
    w_reset, w_update, source, own, w_corr, hidden, motion, w_motion, bias_encoder, bias_update, bias_reset, bias_cand, bias_head,
    pairs, wc, h_first, h_last, s_flat, hidden_here, motion_here, begun, small, re_old, re_new, update_here,
    tt, reset_here, flat, wide, arrived
):
    copies = [
        pltpu.make_async_copy(w_reset, reset_here, arrived.at[0]),
        pltpu.make_async_copy(w_update, update_here, arrived.at[1]),
    ]
    for copy in copies:
        copy.start()
    planes, rows = source.shape[:2]
    h_first[...] = hidden[:2]
    h_last[...] = hidden[planes - 2 :]
    hidden_here[...] = hidden[...]
    motion_here[...] = motion[...]
    width, outs = hidden.shape[2], motion.shape[2]
    for n, row in enumerate((bias_encoder, bias_update, bias_reset, bias_cand)):
        small[n : n + 1, :width] = row[...]
    for n in range(w_motion.shape[0]):
        small[4 + n : 5 + n, :width] = w_motion[n : n + 1, :]
    shift = column(bias_head[...])
    for z in range(planes):
        for y in range(rows):
            s_flat[z, :, y * LANES : (y + 1) * LANES] = source[z, y]
            begun[z, y] = jnp.zeros(begun.shape[2:], F32)
            begun[z, y, :outs] = motion[z, y] + shift
    at = lax.broadcasted_iota(jnp.int32, (w_corr.shape[1], 49 * 8), 0)
    to = lax.broadcasted_iota(jnp.int32, (w_corr.shape[1], 49 * 8), 1)
    pick = ((to & 7) < 7) & (at == (to >> 3) * 7 + (to & 7))
    wc[...] = jnp.dot(w_corr[...], jnp.where(pick, 1.0, 0.0).astype(BF16), preferred_element_type=F32).astype(BF16)
    put_block(tt, own, None, 3, 3)
    corr_part("own", planes, rows, tt, s_flat, pairs)
    copies[0].wait()
    lay_out(width, reset_here, re_old, re_new, flat, wide)
    copies[1].wait()


def corr_face_body(place, s_flat, low, high, mate, other, pairs, tt):
    planes, rows = s_flat.shape[0], s_flat.shape[2] // LANES
    odd = place[3]
    put_block(tt, low, place[0] == 1, 3, 0)
    put_block(tt, high, place[1] == 1, 3, 3 + planes)
    put_block(tt, mate, None, (3 + rows) * (1 - odd), 3)
    put_block(tt, other, place[2] == 1, (3 + rows) * odd, 3)

    corr_part("face", planes, rows, tt, s_flat, pairs)


def corr_corner_body(
    place, s_flat, motion, small, own_pairs, face_pairs, low_mate, low_other, high_mate, high_other, wc,
    enc, enc_first, enc_last, tt, pairs
):
    planes, rows, outs = motion.shape[:3]
    width = enc.shape[2]
    odd = place[3]
    mate_at, other_at = (3 + rows) * (1 - odd), (3 + rows) * odd
    put_block(tt, low_mate, place[0] == 1, mate_at, 0)
    put_block(tt, low_other, place[0] + place[2] == 2, other_at, 0)
    put_block(tt, high_mate, place[1] == 1, mate_at, 3 + planes)
    put_block(tt, high_other, place[1] + place[2] == 2, other_at, 3 + planes)
    shift = column(small[0:1, :width])
    moves = [column(small[4 + k : 5 + k, :width]) for k in range(outs)]
    corr_part("corner", planes, rows, tt, s_flat, pairs)
    scale = s_flat.shape[1] ** (-0.5)
    parts = {"own": own_pairs, "face": face_pairs, "corner": pairs}
    for z, got in enumerate(encode(planes, rows, scale, parts, wc)):
        for y in range(rows):
            total = got[:, y * LANES : (y + 1) * LANES]
            for k, move in enumerate(moves):
                total = total + move * motion[z, y, k : k + 1, :]
            value = jnp.maximum(total + shift, 0.0).astype(BF16)
            enc[z, y] = value
            if z < 2:
                enc_first[z, y] = value
            if z >= planes - 2:
                enc_last[z - planes + 2, y] = value


def pack_body(place, own, low, high, to_mate, to_other):
    width = to_mate.shape[1]
    planes, rows = own.shape[:2]
    odd = place[3]
    for y in range(width):
        mate_at, other_at = (rows - width) * (1 - odd) + y, (rows - width) * odd + y
        first = 0
        for block in (low, own, high):
            to_mate[first : first + block.shape[0], y] = block[:, mate_at]
            to_other[first : first + block.shape[0], y] = block[:, other_at]
            first += block.shape[0]


def rows_of(place, low, own, high, width, name, from_hbm=()):
    planes = low.shape[0] + own.shape[0] + high.shape[0]
    out = jax.ShapeDtypeStruct((planes, width) + own.shape[2:], own.dtype)
    return call(pack_body, (out, out), [], (own, low, high), name, 6, place, from_hbm)


def taps(field, z, row, rows):
    wide = rows * LANES
    got = []
    for a in range(3):
        for b in range(3):
            got.append(field[z + a, :, (row + b) * LANES : (row + b) * LANES + wide])
    return got + [jnp.zeros((32, wide), BF16)]


def side_by_side(field, planes, row, rows):
    return [jnp.concatenate(parts, axis=1) for parts in zip(*[taps(field, z, row, rows) for z in planes])]


def conv(weight, rhs, rows):
    three = jnp.dot(weight, jnp.concatenate(rhs, axis=0), preferred_element_type=F32)
    width = three.shape[0] // 3
    cell = lax.broadcasted_iota(jnp.int32, (width, LANES), 1)
    out = []
    for y in range(rows):
        at = slice(y * LANES, (y + 1) * LANES)
        before = jnp.where(cell == 0, 0.0, pltpu.roll(three[:width, at], 1, 1))
        after = jnp.where(cell == LANES - 1, 0.0, pltpu.roll(three[2 * width :, at], LANES - 1, 1))
        out.append(three[width : 2 * width, at] + before + after)
    return out


def fill(place, field, own, z0, z1, mate, other):
    planes, rows, width = own.shape[:3]
    odd = place[3]
    low, high, along = place[0] == 1, place[1] == 1, place[2] == 1

    def store(plane, y, value):
        at = y * LANES if isinstance(y, int) else pl.multiple_of(y * LANES, LANES)
        field[plane, :, pl.ds(at, LANES)] = value

    def mates(over):
        for plane in over:
            for y in range(2):
                store(plane, y + (rows + 2) * (1 - odd), mate(plane, y))

    def others(over, inside=True):
        for plane in over:
            for y in range(2):
                value = other(plane, y) if inside else jnp.zeros((width, LANES), BF16)
                store(plane, y + (rows + 2) * odd, value)

    def outside(over):
        for plane in over:
            field[plane] = jnp.zeros(field.shape[1:], BF16)

    for plane in range(planes):
        for y in range(rows):
            store(plane + 2, y + 2, own[plane, y])
    middle = range(2, planes + 2)
    mates(middle)
    pl.when(along)(lambda: others(middle))
    pl.when(jnp.logical_not(along))(lambda: others(middle, False))
    for ok, block, first in ((low, z0, 0), (high, z1, planes + 2)):
        over = range(first, first + 2)

        def inner(block=block, first=first, over=over):
            for plane in over:
                for y in range(rows):
                    store(plane, y + 2, block[plane - first, y])
            mates(over)

        pl.when(ok)(inner)
        pl.when(jnp.logical_not(ok))(lambda over=over: outside(over))
        pl.when(jnp.logical_and(ok, along))(lambda over=over: others(over))
        pl.when(jnp.logical_and(ok, jnp.logical_not(along)))(lambda over=over: others(over, False))


def old_body(place, hidden, small, hz0, hz1, h_mate, h_other, a_up, a_re, update_out, reset_out, near_out, field):
    planes, rows = hidden.shape[:2]
    fill(place, field, hidden, hz0, hz1, lambda plane, y: h_mate[plane, y], lambda plane, y: h_other[plane, y])
    width = hidden.shape[2]
    up_shift, re_shift = column(small[1:2, :width]), column(small[2:3, :width])

    for z in range(planes + 2):
        near_out[z] = field[z + 1, :, LANES : (rows + 3) * LANES]
    for n, got in enumerate(conv(a_re[...], side_by_side(field, range(planes + 2), 0, rows + 2), (planes + 2) * (rows + 2))):
        reset_out[n // (rows + 2), n % (rows + 2)] = got + re_shift
    for n, got in enumerate(conv(a_up[...], side_by_side(field, range(1, planes + 1), 1, rows), planes * rows)):
        update_out[n // rows, n % rows] = got + up_shift


def new_states(planes, rows, small, near, update_old, field, gated, a_up, a_ca_old, a_ca_new):
    width = near.shape[1]
    ca_shift = column(small[3:4, :width])
    new_taps = side_by_side(field, [z + 1 for z in planes], 1, rows)
    update = conv(a_up[...], new_taps, len(planes) * rows)
    both = jnp.concatenate([a_ca_old[...], a_ca_new[...]], axis=1)
    cand = conv(both, side_by_side(gated, planes, 0, rows) + new_taps, len(planes) * rows)
    for n in range(len(planes) * rows):
        z, y = planes[n // rows], n % rows
        gate = jax.nn.sigmoid(update[n] + update_old[z, y])
        new = jnp.tanh(cand[n] + ca_shift)
        old = near[z + 1, :, (y + 1) * LANES : (y + 2) * LANES].astype(F32)
        yield z, y, ((1.0 - gate) * old + gate * new).astype(BF16)


def head_parts(head, state, planes, rows):
    cell = lax.broadcasted_iota(jnp.int32, (8, LANES), 1)
    sums, parts = {}, {}
    for n, z in enumerate(planes):
        prod = jnp.dot(head[...], state[n], preferred_element_type=F32)
        for y in range(rows):
            for a in range(3):
                for b in range(3):
                    for c in range(3):
                        t = a * 9 + b * 3 + c
                        piece = prod[t * 8 : t * 8 + 8, y * LANES : (y + 1) * LANES]
                        slot = sums.setdefault((z + 2 - a, y + 2 - b), [None] * 3)
                        slot[c] = piece if slot[c] is None else slot[c] + piece
    for key, (before, same, after) in sums.items():
        before = jnp.where(cell == 0, 0.0, pltpu.roll(before, 1, 1))
        after = jnp.where(cell == LANES - 1, 0.0, pltpu.roll(after, LANES - 1, 1))
        parts[key] = same + before + after
    return parts


def outer_planes(planes):
    return sorted({0, planes - 1})


def gru_outer_body(
    place, begun, small, near, update_old, reset_old, enc, ez0, ez1, e_mate, e_other, a_up, a_re, a_ca_old, a_ca_new, head,
    part_low, part_out, part_high, field, gated, outer, state
):
    planes, rows = enc.shape[:2]
    fill(place, field, enc, ez0, ez1, lambda plane, y: e_mate[plane, y], lambda plane, y: e_other[plane, y])
    every = range(planes + 2)
    for n, got in enumerate(conv(a_re[...], side_by_side(field, every, 0, rows + 2), (planes + 2) * (rows + 2))):
        z, y = n // (rows + 2), n % (rows + 2)
        at = slice(y * LANES, (y + 1) * LANES)
        gate = jax.nn.sigmoid(got + reset_old[z, y])
        gated[z, :, at] = (gate * near[z, :, at].astype(F32)).astype(BF16)

    ends = outer_planes(planes)
    for z, y, got in new_states(ends, rows, small, near, update_old, field, gated, a_up, a_ca_old, a_ca_new):
        outer[ends.index(z), y] = got
        state[ends.index(z), :, y * LANES : (y + 1) * LANES] = got

    parts = head_parts(head, state, ends, rows)
    for z in range(planes + 2):
        for y in range(rows + 2):
            total = parts.get((z, y))
            if 0 < z <= planes and 0 < y <= rows:
                total = begun[z - 1, y - 1] if total is None else total + begun[z - 1, y - 1]
            if total is None:
                total = jnp.zeros(part_out.shape[2:], F32)
            if z == 0:
                part_low[0, y] = total
            elif z == planes + 1:
                part_high[0, y] = total
            else:
                part_out[z - 1, y] = total


def gru_inner_body(
    small, near, update_old, field, gated, a_up, a_ca_old, a_ca_new, head, part, outer, state_out, part_out, state
):
    planes, rows = state_out.shape[:2]
    ends = outer_planes(planes)
    inner = [z for z in range(planes) if z not in ends]
    for n, z in enumerate(ends):
        state_out[z] = outer[n]
    part_out[...] = part[...]
    for z, y, got in new_states(inner, rows, small, near, update_old, field, gated, a_up, a_ca_old, a_ca_new):
        state_out[z, y] = got
        state[inner.index(z), :, y * LANES : (y + 1) * LANES] = got
    for (z, y), total in head_parts(head, state, inner, rows).items():
        part_out[z - 1, y] = part[z - 1, y] + total


def mix_body(place, part, low, high, mine, to_mate, to_other):
    planes, rows = mine.shape[:2]
    odd = place[3]
    mate_at, other_at = (rows + 1) * (1 - odd), (rows + 1) * odd

    def added(z, at):
        total = part[z, at]
        if z == 0:
            total = total + jnp.where(place[0] == 1, low[0, at], 0.0)
        if z == planes - 1:
            total = total + jnp.where(place[1] == 1, high[0, at], 0.0)
        return total

    for z in range(planes):
        for y in range(rows):
            mine[z, y] = added(z, y + 1)
        to_mate[z, 0] = added(z, mate_at)
        to_other[z, 0] = added(z, other_at)


def on_device(
    source, target, hidden, motion, w_corr, w_motion, bias_encoder, w_update, bias_update,
    w_reset, bias_reset, w_cand, bias_cand, w_head, bias_head
):
    planes, rows, channels, cells = source.shape
    width = hidden.shape[2]
    wide = rows * LANES
    place = inside()

    t_low, t_high = planes_around(target[:3], target[-3:])
    to_mate, to_other = edges(target, 3)
    t_other = rows_of_other(to_other)

    target_rows = pltpu.VMEM((rows + 6, planes + 6, LANES, channels), BF16)
    made = jax.ShapeDtypeStruct
    pairs = {part: made((len(slots_of(part, planes, rows)), 8, cells), F32) for part in ("own", "face", "corner")}
    two = made((2, rows, width, cells), BF16)
    eight = made((planes, rows, 8, cells), F32)
    laid = pltpu.HBM((3 * width, 7 * LANES), BF16)
    biases = [b[None, :] for b in (bias_encoder, bias_update, bias_reset, bias_cand, bias_head)]
    own, wc, h_first, h_last, s_flat, hidden_here, motion_here, begun, small, re_old, re_new, update_here = call(
        own_body,
        (pairs["own"], made((width, 49 * 8), BF16), two, two, made((planes, channels, wide), BF16))
        + (made(hidden.shape, BF16), made(motion.shape, F32), eight, made((8, LANES), F32), laid, laid)
        + (made(w_update.shape, BF16),),
        [target_rows, pltpu.VMEM(w_reset.shape, BF16)] + lay_out_scratch(width) + [pltpu.SemaphoreType.DMA((2,))],
        [w_reset, w_update, source, target, w_corr, hidden, motion, w_motion.T] + biases,
        "own",
        14,
        from_hbm=(pltpu.HBM,) * 2 + (pltpu.VMEM,) * 11,
    )
    t_low, to_mate, own = lax.optimization_barrier((t_low, to_mate, own))
    t_mate = rows_of_mate(to_mate)
    t_low_mate, t_low_other = rows_around(*edges(t_low, 3))
    update_here, t_low = lax.optimization_barrier((update_here, t_low))
    up_old, up_new = call(
        update_body, (laid, laid), lay_out_scratch(width), (update_here,), "lay_out_update", 8
    )
    t_high, up_new = lax.optimization_barrier((t_high, up_new))
    t_high_mate, t_high_other = rows_around(*edges(t_high, 3))
    h_first, h_last, t_low, t_high = lax.optimization_barrier((h_first, h_last, t_low, t_high))
    h_low, h_high = planes_around(h_first, h_last)
    face = call(
        corr_face_body, pairs["face"], [target_rows], (s_flat, t_low, t_high, t_mate, t_other), "face", 9, place
    )

    enc, enc_first, enc_last = call(
        corr_corner_body,
        (made(hidden.shape, BF16), two, two),
        [target_rows] + [pltpu.VMEM(pairs["corner"].shape, F32)],
        (s_flat, motion_here, small)
        + (own, face, t_low_mate, t_low_other, t_high_mate, t_high_other, wc),
        "corner",
        10,
        place,
    )
    e_low, e_high = planes_around(enc_first, enc_last)
    taps_head, enc = lax.optimization_barrier((jnp.transpose(w_head, (1, 0, 2)), enc))
    ca_old, ca_new, head = call(
        cand_body,
        (laid, laid, pltpu.HBM((27 * 8, width), BF16)),
        lay_out_scratch(width) + [pltpu.VMEM((27 * 8, LANES), F32)],
        (w_cand, taps_head),
        "lay_out_cand",
        8,
        from_hbm=(pltpu.VMEM,) * 2,
    )
    e_low, ca_new = lax.optimization_barrier((e_low, ca_new))
    h_low, h_high, enc = lax.optimization_barrier((h_low, h_high, enc))
    h_mate, h_other = rows_around(*rows_of(place, h_low, hidden_here, h_high, 2, "pack_hidden"))
    field = pltpu.VMEM((planes + 4, width, (rows + 4) * LANES), BF16)
    update_old, reset_old, near = call(
        old_body,
        (
            jax.ShapeDtypeStruct((planes, rows, width, cells), F32),
            jax.ShapeDtypeStruct((planes + 2, rows + 2, width, cells), F32),
            jax.ShapeDtypeStruct((planes + 2, width, (rows + 2) * LANES), BF16),
        ),
        [field],
        (hidden_here, small, h_low, h_high, h_mate, h_other, up_old, re_old),
        "old",
        10,
        place,
    )
    e_mate, e_other = rows_around(*rows_of(place, e_low, enc, e_high, 2, "pack_encoded"))

    ring = lambda n: jax.ShapeDtypeStruct((n, rows + 2, 8, cells), F32)
    ends = len(outer_planes(planes))
    part_low, part, part_high, e_field, gated, outer = call(
        gru_outer_body,
        (ring(1), ring(planes), ring(1), made(field.shape, BF16))
        + (made((planes + 2, width, (rows + 2) * LANES), BF16), made((ends, rows, width, cells), BF16)),
        [pltpu.VMEM((ends, width, wide), BF16)],
        (begun, small, near, update_old, reset_old, enc, e_low, e_high, e_mate, e_other)
        + (up_new, re_new, ca_old, ca_new, head),
        "gru_outer",
        12,
        place,
    )
    low, high = planes_around(part_low, part_high)
    state_out, part = call(
        gru_inner_body,
        (pltpu.HBM(hidden.shape, BF16), ring(planes)),
        [pltpu.VMEM((planes - ends, width, wide), BF16)],
        (small, near, update_old, e_field, gated, up_new, ca_old, ca_new, head, part, outer),
        "gru_inner",
        12,
    )
    row = jax.ShapeDtypeStruct((planes, 1, 8, cells), F32)
    mine, to_mate, to_other = call(
        mix_body,
        (jax.ShapeDtypeStruct((planes, rows, 8, cells), F32), row, row),
        [],
        (part, low, high),
        "mix",
        4,
        place,
    )
    mate, other = rows_around(to_mate, to_other)
    other = jnp.where(place[2] == 1, other, 0.0)
    odd = place[3] == 1
    below, above = jnp.where(odd, mate, other), jnp.where(odd, other, mate)
    row = lax.broadcasted_iota(jnp.int32, mine.shape, 1)
    total = mine + jnp.where(row == 0, below, 0.0) + jnp.where(row == rows - 1, above, 0.0)
    motion_out = total[:, :, : motion.shape[2]]
    return state_out, motion_out


def solution(mesh):
    split = P("gz", "gy", None, None)
    return jax.shard_map(
        on_device,
        mesh=mesh,
        in_specs=(split,) * 4 + (P(),) * 11,
        out_specs=(split, split),
        check_vma=False,
    )
```

```python
import functools

import jax
import jax.numpy as jnp
from jax import lax
from jax.experimental import pallas as pl
from jax.experimental.pallas import tpu as pltpu
from jax.sharding import PartitionSpec as P

F32 = jnp.float32
BF16 = jnp.bfloat16
LANES = 128
MIB = 1024 * 1024


def around(block, axis, step):
    count = lax.axis_size(axis)
    return lax.ppermute(block, axis, [(i, (i + step) % count) for i in range(count)])


def planes_around(first, last):
    return around(last, "gz", 1), around(first, "gz", -1)


def rows_of_mate(to_mate):
    count = lax.axis_size("gy")
    return lax.ppermute(to_mate, "gy", [(i, i ^ 1) for i in range(count)])


def rows_of_other(to_other):
    count = lax.axis_size("gy")
    return lax.ppermute(to_other, "gy", [(i, ((i + 1) ^ 1) - 1) for i in range(1, count - 1)])


def rows_around(to_mate, to_other):
    other = rows_of_other(to_other)
    return rows_of_mate(to_mate), other


def edges(block, width):
    rows = block.shape[1]
    if rows == width:
        return block, block
    odd = lax.axis_index("gy") % 2
    to_mate = lax.dynamic_slice_in_dim(block, (rows - width) * (1 - odd), width, axis=1)
    return to_mate, lax.dynamic_slice_in_dim(block, (rows - width) * odd, width, axis=1)


def inside():
    z, y = lax.axis_index("gz"), lax.axis_index("gy")
    odd = y % 2
    end = jnp.where(odd == 1, lax.axis_size("gy") - 1, 0)
    return jnp.stack([z > 0, z < lax.axis_size("gz") - 1, y != end, odd == 1]).astype(jnp.int32)


def vmem(count):
    return [pl.BlockSpec(memory_space=pltpu.VMEM)] * count


def call(body, out_shape, scratch, args, name, mib, place=None, from_hbm=(), kept=True):
    struct = lambda o: isinstance(o, jax.ShapeDtypeStruct)
    in_specs = vmem(len(args))
    for n, given in enumerate(from_hbm):
        in_specs[n] = pl.BlockSpec(memory_space=given)
    args = [pltpu.with_memory_space_constraint(a, pltpu.HBM if n < len(from_hbm) else pltpu.VMEM) for n, a in enumerate(args)]
    if place is not None:
        args = [place] + args
        in_specs = [pl.BlockSpec(memory_space=pltpu.SMEM)] + in_specs
    return pl.pallas_call(
        body,
        out_shape=jax.tree.map(lambda o: pltpu.VMEM(o.shape, o.dtype) if kept and struct(o) else o, out_shape),
        in_specs=in_specs,
        out_specs=jax.tree.map(lambda _: pl.BlockSpec(memory_space=pltpu.VMEM), out_shape),
        scratch_shapes=scratch,
        compiler_params=pltpu.CompilerParams(vmem_limit_bytes=mib * MIB),
        cost_estimate=pl.CostEstimate(flops=1000, bytes_accessed=1000, transcendentals=0),
        name=name,
    )(*args)


def lay_out(width, weight, first_out, last_out, flat, wide):
    pieces = width * 2 * width // LANES
    pitch = pieces + 1
    half = width // 2
    lane = lax.broadcasted_iota(jnp.int32, (half, LANES), 1)

    def turn(value, by):
        return pltpu.roll(value, by, 1)

    def packed(parts):
        made = []
        for first in range(0, 9, 4):
            group = parts[first : first + 4]
            if len(group) == 1:
                made.append(jnp.where(lane < 96, group[0], 0.0))
                continue
            one, two = turn(group[1], 96), turn(group[2], 64)
            made.append(jnp.where(lane < 96, group[0], one))
            made.append(jnp.where(lane < 64, one, two))
            made.append(jnp.where(lane < 32, two, turn(group[3], 32)))
        return made

    def spread(j, carry):
        got = weight[:, pl.ds(pl.multiple_of(j * LANES, LANES), LANES)].astype(F32)
        for first in range(0, 27, 8):
            size = min(8, 27 - first)
            flat[pl.ds(j + first * pitch, size, stride=pitch), :] = got[first : first + size]
        return carry

    lax.fori_loop(0, pieces, spread, 0, unroll=8)

    for c in range(3):
        rows = [[], [], [], []]
        for ab in range(9):
            first, mid, last = [flat[pl.ds((ab * 3 + c) * pitch + k, half, stride=3), :] for k in range(3)]
            rows[0].append(first)
            rows[1].append(turn(jnp.where(lane < 64, last, mid), 64))
            rows[2].append(turn(jnp.where(lane >= 96, first, mid), 32))
            rows[3].append(turn(last, 96))
        for part in range(4):
            for k, chunk in enumerate(packed(rows[part])):
                wide[part // 2, k, pl.ds(c * width + part % 2, half, stride=2), :] = chunk
    for part, out in enumerate((first_out, last_out)):
        for chunk in range(7):
            out[:, chunk * LANES : (chunk + 1) * LANES] = wide[part, chunk].astype(BF16)


def lay_out_scratch(width):
    pitch = width * 2 * width // LANES + 1
    return [pltpu.VMEM((32 * pitch, LANES), F32), pltpu.VMEM((2, 7, 3 * width, LANES), F32)]


def update_body(weight, first_out, last_out, flat, wide):
    lay_out(first_out.shape[0] // 3, weight, first_out, last_out, flat, wide)


def cand_body(weight, head, first_out, last_out, head_out, flat, wide, eights):
    width = head.shape[2]
    lay_out(width, weight, first_out, last_out, flat, wide)
    eights[...] = jnp.zeros_like(eights)
    for o in range(head.shape[0]):
        eights[pl.ds(o, 27, stride=8), :width] = head[o].astype(F32)
    head_out[...] = eights[:, :width].astype(BF16)


def held_rows(part, planes, rows):
    def held(j):
        if 3 <= j < 3 + rows:
            return {"own": [(3, 3 + planes)], "face": [(0, 3), (3 + planes, 6 + planes)], "corner": []}[part]
        return {"own": [], "face": [(3, 3 + planes)], "corner": [(0, 3), (3 + planes, 6 + planes)]}[part]

    return held


def slots_of(part, planes, rows):
    slots = {}
    held = held_rows(part, planes, rows)
    for z in range(planes):
        for j in range(rows + 6):
            for first, last in held(j):
                for plane in range(max(z, first), min(z + 7, last)):
                    for y in range(rows):
                        if 0 <= j - y <= 6:
                            slots[z, y, (plane - z) * 7 + j - y] = len(slots)
    return slots


def corr_part(part, planes_out, rows_out, tt, s_flat, pairs):
    channels = s_flat.shape[1]
    sub = lax.broadcasted_iota(jnp.int32, (8, LANES), 0)
    cell = lax.broadcasted_iota(jnp.int32, (8, LANES), 1)
    block_of = (cell + 4 - sub + 8) // 8 - 1
    held, slots = held_rows(part, planes_out, rows_out), slots_of(part, planes_out, rows_out)

    for z in range(planes_out):
        for j in range(rows_out + 6):
            ys = [y for y in range(rows_out) if 0 <= j - y <= 6]
            lo, hi = ys[0] * LANES, (ys[-1] + 1) * LANES
            for first, last in held(j):
                first, last = max(z, first), min(z + 7, last)
                if first >= last:
                    continue
                lhs = tt[j, first:last].reshape((last - first) * LANES, channels)
                prod = jnp.dot(lhs, s_flat[z, :, lo:hi], preferred_element_type=F32)
                for plane in range(first, last):
                    for n, y in enumerate(ys):
                        got = jnp.zeros((8, LANES), F32)
                        for k in range(LANES // 8):
                            at = (plane - first) * LANES + 8 * k
                            piece = prod[at : at + 8, n * LANES : (n + 1) * LANES]
                            got = jnp.where(block_of == k, piece, got)
                        pairs[slots[z, y, (plane - z) * 7 + j - y]] = got


def encode(planes, rows, scale, parts, wc):
    wide = rows * LANES
    found = {}
    for part, pairs in parts.items():
        found.update({key: (pairs, slot) for key, slot in slots_of(part, planes, rows).items()})
    turn = (3 - lax.broadcasted_iota(jnp.int32, (1, 8, LANES), 2)) & 7
    turn = jnp.concatenate([turn] * rows, axis=2)
    columns = []
    for z in range(planes):
        made = []
        for pair in range(49):
            row = []
            for y in range(rows):
                pairs, slot = found[z, y, pair]
                row.append(pairs[slot])
            made.append(jnp.concatenate(row, axis=1)[None])
        got = jnp.concatenate(made, axis=0)
        for bit in (1, 2, 4):
            got = jnp.where((turn & bit) != 0, pltpu.roll(got, bit, 1), got)
        columns.append((got * scale).reshape(49 * 8, wide).astype(BF16))
    sums = jnp.dot(wc[...], jnp.concatenate(columns, axis=1), preferred_element_type=F32)
    return [sums[:, z * wide : (z + 1) * wide] for z in range(planes)]


def put_block(tt, block, ok, row, plane):
    def store(value):
        for p in range(block.shape[0]):
            for y in range(block.shape[1]):
                tt[row + y, plane + p] = value(p, y)

    if ok is None:
        store(lambda p, y: block[p, y].T)
        return

    @pl.when(ok)
    def _():
        store(lambda p, y: block[p, y].T)

    @pl.when(jnp.logical_not(ok))
    def _():
        store(lambda p, y: jnp.zeros(tt.shape[2:], BF16))


def column(row):
    return jnp.broadcast_to(row, (LANES, row.shape[1])).T


def own_body(
    w_reset, w_update, source, own, w_corr, hidden, motion, w_motion, bias_encoder, bias_update, bias_reset, bias_cand, bias_head,
    pairs, wc, h_first, h_last, s_flat, hidden_here, motion_here, begun, small, re_old, re_new, update_here,
    tt, reset_here, flat, wide, arrived
):
    copies = [
        pltpu.make_async_copy(w_reset, reset_here, arrived.at[0]),
        pltpu.make_async_copy(w_update, update_here, arrived.at[1]),
    ]
    for copy in copies:
        copy.start()
    planes, rows = source.shape[:2]
    h_first[...] = hidden[:2]
    h_last[...] = hidden[planes - 2 :]
    hidden_here[...] = hidden[...]
    motion_here[...] = motion[...]
    width, outs = hidden.shape[2], motion.shape[2]
    for n, row in enumerate((bias_encoder, bias_update, bias_reset, bias_cand)):
        small[n : n + 1, :width] = row[...]
    for n in range(w_motion.shape[0]):
        small[4 + n : 5 + n, :width] = w_motion[n : n + 1, :]
    shift = column(bias_head[...])
    for z in range(planes):
        for y in range(rows):
            s_flat[z, :, y * LANES : (y + 1) * LANES] = source[z, y]
            begun[z, y] = jnp.zeros(begun.shape[2:], F32)
            begun[z, y, :outs] = motion[z, y] + shift
    at = lax.broadcasted_iota(jnp.int32, (w_corr.shape[1], 49 * 8), 0)
    to = lax.broadcasted_iota(jnp.int32, (w_corr.shape[1], 49 * 8), 1)
    pick = ((to & 7) < 7) & (at == (to >> 3) * 7 + (to & 7))
    wc[...] = jnp.dot(w_corr[...], jnp.where(pick, 1.0, 0.0).astype(BF16), preferred_element_type=F32).astype(BF16)
    put_block(tt, own, None, 3, 3)
    corr_part("own", planes, rows, tt, s_flat, pairs)
    copies[0].wait()
    lay_out(width, reset_here, re_old, re_new, flat, wide)
    copies[1].wait()


def corr_face_body(place, s_flat, low, high, mate, other, pairs, tt):
    planes, rows = s_flat.shape[0], s_flat.shape[2] // LANES
    odd = place[3]
    put_block(tt, low, place[0] == 1, 3, 0)
    put_block(tt, high, place[1] == 1, 3, 3 + planes)
    put_block(tt, mate, None, (3 + rows) * (1 - odd), 3)
    put_block(tt, other, place[2] == 1, (3 + rows) * odd, 3)

    corr_part("face", planes, rows, tt, s_flat, pairs)


def corr_corner_body(
    place, s_flat, motion, small, own_pairs, face_pairs, low_mate, low_other, high_mate, high_other, wc,
    enc, enc_first, enc_last, tt, pairs
):
    planes, rows, outs = motion.shape[:3]
    width = enc.shape[2]
    odd = place[3]
    mate_at, other_at = (3 + rows) * (1 - odd), (3 + rows) * odd
    put_block(tt, low_mate, place[0] == 1, mate_at, 0)
    put_block(tt, low_other, place[0] + place[2] == 2, other_at, 0)
    put_block(tt, high_mate, place[1] == 1, mate_at, 3 + planes)
    put_block(tt, high_other, place[1] + place[2] == 2, other_at, 3 + planes)
    shift = column(small[0:1, :width])
    moves = [column(small[4 + k : 5 + k, :width]) for k in range(outs)]
    corr_part("corner", planes, rows, tt, s_flat, pairs)
    scale = s_flat.shape[1] ** (-0.5)
    parts = {"own": own_pairs, "face": face_pairs, "corner": pairs}
    for z, got in enumerate(encode(planes, rows, scale, parts, wc)):
        for y in range(rows):
            total = got[:, y * LANES : (y + 1) * LANES]
            for k, move in enumerate(moves):
                total = total + move * motion[z, y, k : k + 1, :]
            value = jnp.maximum(total + shift, 0.0).astype(BF16)
            enc[z, y] = value
            if z < 2:
                enc_first[z, y] = value
            if z >= planes - 2:
                enc_last[z - planes + 2, y] = value


def pack_body(place, own, low, high, to_mate, to_other):
    width = to_mate.shape[1]
    planes, rows = own.shape[:2]
    odd = place[3]
    for y in range(width):
        mate_at, other_at = (rows - width) * (1 - odd) + y, (rows - width) * odd + y
        first = 0
        for block in (low, own, high):
            to_mate[first : first + block.shape[0], y] = block[:, mate_at]
            to_other[first : first + block.shape[0], y] = block[:, other_at]
            first += block.shape[0]


def rows_of(place, low, own, high, width, name, from_hbm=()):
    planes = low.shape[0] + own.shape[0] + high.shape[0]
    out = jax.ShapeDtypeStruct((planes, width) + own.shape[2:], own.dtype)
    return call(pack_body, (out, out), [], (own, low, high), name, 6, place, from_hbm)


def taps(field, z, row, rows):
    wide = rows * LANES
    got = []
    for a in range(3):
        for b in range(3):
            got.append(field[z + a, :, (row + b) * LANES : (row + b) * LANES + wide])
    return got + [jnp.zeros((32, wide), BF16)]


def side_by_side(field, planes, row, rows):
    return [jnp.concatenate(parts, axis=1) for parts in zip(*[taps(field, z, row, rows) for z in planes])]


def conv(weight, rhs, rows):
    three = jnp.dot(weight, jnp.concatenate(rhs, axis=0), preferred_element_type=F32)
    width = three.shape[0] // 3
    cell = lax.broadcasted_iota(jnp.int32, (width, LANES), 1)
    out = []
    for y in range(rows):
        at = slice(y * LANES, (y + 1) * LANES)
        before = jnp.where(cell == 0, 0.0, pltpu.roll(three[:width, at], 1, 1))
        after = jnp.where(cell == LANES - 1, 0.0, pltpu.roll(three[2 * width :, at], LANES - 1, 1))
        out.append(three[width : 2 * width, at] + before + after)
    return out


def fill(place, field, own, z0, z1, mate, other):
    planes, rows, width = own.shape[:3]
    odd = place[3]
    low, high, along = place[0] == 1, place[1] == 1, place[2] == 1

    def store(plane, y, value):
        at = y * LANES if isinstance(y, int) else pl.multiple_of(y * LANES, LANES)
        field[plane, :, pl.ds(at, LANES)] = value

    def mates(over):
        for plane in over:
            for y in range(2):
                store(plane, y + (rows + 2) * (1 - odd), mate(plane, y))

    def others(over, inside=True):
        for plane in over:
            for y in range(2):
                value = other(plane, y) if inside else jnp.zeros((width, LANES), BF16)
                store(plane, y + (rows + 2) * odd, value)

    def outside(over):
        for plane in over:
            field[plane] = jnp.zeros(field.shape[1:], BF16)

    for plane in range(planes):
        for y in range(rows):
            store(plane + 2, y + 2, own[plane, y])
    middle = range(2, planes + 2)
    mates(middle)
    pl.when(along)(lambda: others(middle))
    pl.when(jnp.logical_not(along))(lambda: others(middle, False))
    for ok, block, first in ((low, z0, 0), (high, z1, planes + 2)):
        over = range(first, first + 2)

        def inner(block=block, first=first, over=over):
            for plane in over:
                for y in range(rows):
                    store(plane, y + 2, block[plane - first, y])
            mates(over)

        pl.when(ok)(inner)
        pl.when(jnp.logical_not(ok))(lambda over=over: outside(over))
        pl.when(jnp.logical_and(ok, along))(lambda over=over: others(over))
        pl.when(jnp.logical_and(ok, jnp.logical_not(along)))(lambda over=over: others(over, False))


def old_body(place, hidden, small, hz0, hz1, h_mate, h_other, a_up, a_re, update_out, reset_out, near_out, field):
    planes, rows = hidden.shape[:2]
    fill(place, field, hidden, hz0, hz1, lambda plane, y: h_mate[plane, y], lambda plane, y: h_other[plane, y])
    width = hidden.shape[2]
    up_shift, re_shift = column(small[1:2, :width]), column(small[2:3, :width])

    for z in range(planes + 2):
        near_out[z] = field[z + 1, :, LANES : (rows + 3) * LANES]
    for n, got in enumerate(conv(a_re[...], side_by_side(field, range(planes + 2), 0, rows + 2), (planes + 2) * (rows + 2))):
        reset_out[n // (rows + 2), n % (rows + 2)] = got + re_shift
    for n, got in enumerate(conv(a_up[...], side_by_side(field, range(1, planes + 1), 1, rows), planes * rows)):
        update_out[n // rows, n % rows] = got + up_shift


def new_states(planes, rows, small, near, update_old, field, gated, a_up, a_ca_old, a_ca_new):
    width = near.shape[1]
    ca_shift = column(small[3:4, :width])
    new_taps = side_by_side(field, [z + 1 for z in planes], 1, rows)
    update = conv(a_up[...], new_taps, len(planes) * rows)
    both = jnp.concatenate([a_ca_old[...], a_ca_new[...]], axis=1)
    cand = conv(both, side_by_side(gated, planes, 0, rows) + new_taps, len(planes) * rows)
    for n in range(len(planes) * rows):
        z, y = planes[n // rows], n % rows
        gate = jax.nn.sigmoid(update[n] + update_old[z, y])
        new = jnp.tanh(cand[n] + ca_shift)
        old = near[z + 1, :, (y + 1) * LANES : (y + 2) * LANES].astype(F32)
        yield z, y, ((1.0 - gate) * old + gate * new).astype(BF16)


def head_parts(head, state, planes, rows):
    cell = lax.broadcasted_iota(jnp.int32, (8, LANES), 1)
    sums, parts = {}, {}
    for n, z in enumerate(planes):
        prod = jnp.dot(head[...], state[n], preferred_element_type=F32)
        for y in range(rows):
            for a in range(3):
                for b in range(3):
                    for c in range(3):
                        t = a * 9 + b * 3 + c
                        piece = prod[t * 8 : t * 8 + 8, y * LANES : (y + 1) * LANES]
                        slot = sums.setdefault((z + 2 - a, y + 2 - b), [None] * 3)
                        slot[c] = piece if slot[c] is None else slot[c] + piece
    for key, (before, same, after) in sums.items():
        before = jnp.where(cell == 0, 0.0, pltpu.roll(before, 1, 1))
        after = jnp.where(cell == LANES - 1, 0.0, pltpu.roll(after, LANES - 1, 1))
        parts[key] = same + before + after
    return parts


def outer_planes(planes):
    return sorted({0, planes - 1})


def gru_outer_body(
    place, begun, small, near, update_old, reset_old, enc, ez0, ez1, e_mate, e_other, a_up, a_re, a_ca_old, a_ca_new, head,
    part_low, part_out, part_high, field, gated, outer, state
):
    planes, rows = enc.shape[:2]
    fill(place, field, enc, ez0, ez1, lambda plane, y: e_mate[plane, y], lambda plane, y: e_other[plane, y])
    every = range(planes + 2)
    for n, got in enumerate(conv(a_re[...], side_by_side(field, every, 0, rows + 2), (planes + 2) * (rows + 2))):
        z, y = n // (rows + 2), n % (rows + 2)
        at = slice(y * LANES, (y + 1) * LANES)
        gate = jax.nn.sigmoid(got + reset_old[z, y])
        gated[z, :, at] = (gate * near[z, :, at].astype(F32)).astype(BF16)

    ends = outer_planes(planes)
    for z, y, got in new_states(ends, rows, small, near, update_old, field, gated, a_up, a_ca_old, a_ca_new):
        outer[ends.index(z), y] = got
        state[ends.index(z), :, y * LANES : (y + 1) * LANES] = got

    parts = head_parts(head, state, ends, rows)
    for z in range(planes + 2):
        for y in range(rows + 2):
            total = parts.get((z, y))
            if 0 < z <= planes and 0 < y <= rows:
                total = begun[z - 1, y - 1] if total is None else total + begun[z - 1, y - 1]
            if total is None:
                total = jnp.zeros(part_out.shape[2:], F32)
            if z == 0:
                part_low[0, y] = total
            elif z == planes + 1:
                part_high[0, y] = total
            else:
                part_out[z - 1, y] = total


def gru_inner_body(
    small, near, update_old, field, gated, a_up, a_ca_old, a_ca_new, head, part, outer, state_out, part_out, state
):
    planes, rows = state_out.shape[:2]
    ends = outer_planes(planes)
    inner = [z for z in range(planes) if z not in ends]
    for n, z in enumerate(ends):
        state_out[z] = outer[n]
    part_out[...] = part[...]
    for z, y, got in new_states(inner, rows, small, near, update_old, field, gated, a_up, a_ca_old, a_ca_new):
        state_out[z, y] = got
        state[inner.index(z), :, y * LANES : (y + 1) * LANES] = got
    for (z, y), total in head_parts(head, state, inner, rows).items():
        part_out[z - 1, y] = part[z - 1, y] + total


def mix_body(place, part, low, high, mine, to_mate, to_other):
    planes, rows = mine.shape[:2]
    odd = place[3]
    mate_at, other_at = (rows + 1) * (1 - odd), (rows + 1) * odd

    def added(z, at):
        total = part[z, at]
        if z == 0:
            total = total + jnp.where(place[0] == 1, low[0, at], 0.0)
        if z == planes - 1:
            total = total + jnp.where(place[1] == 1, high[0, at], 0.0)
        return total

    for z in range(planes):
        for y in range(rows):
            mine[z, y] = added(z, y + 1)
        to_mate[z, 0] = added(z, mate_at)
        to_other[z, 0] = added(z, other_at)


def on_device(
    source, target, hidden, motion, w_corr, w_motion, bias_encoder, w_update, bias_update,
    w_reset, bias_reset, w_cand, bias_cand, w_head, bias_head
):
    planes, rows, channels, cells = source.shape
    width = hidden.shape[2]
    wide = rows * LANES
    place = inside()

    t_low, t_high = planes_around(target[:3], target[-3:])
    to_mate, to_other = edges(target, 3)
    t_other = rows_of_other(to_other)

    target_rows = pltpu.VMEM((rows + 6, planes + 6, LANES, channels), BF16)
    made = jax.ShapeDtypeStruct
    pairs = {part: made((len(slots_of(part, planes, rows)), 8, cells), F32) for part in ("own", "face", "corner")}
    two = made((2, rows, width, cells), BF16)
    eight = made((planes, rows, 8, cells), F32)
    laid = pltpu.HBM((3 * width, 7 * LANES), BF16)
    biases = [b[None, :] for b in (bias_encoder, bias_update, bias_reset, bias_cand, bias_head)]
    own, wc, h_first, h_last, s_flat, hidden_here, motion_here, begun, small, re_old, re_new, update_here = call(
        own_body,
        (pairs["own"], made((width, 49 * 8), BF16), two, two, made((planes, channels, wide), BF16))
        + (made(hidden.shape, BF16), made(motion.shape, F32), eight, made((8, LANES), F32), laid, laid)
        + (made(w_update.shape, BF16),),
        [target_rows, pltpu.VMEM(w_reset.shape, BF16)] + lay_out_scratch(width) + [pltpu.SemaphoreType.DMA((2,))],
        [w_reset, w_update, source, target, w_corr, hidden, motion, w_motion.T] + biases,
        "own",
        15,
        from_hbm=(pltpu.HBM,) * 2 + (pltpu.VMEM,) * 11,
    )
    t_low, to_mate, own = lax.optimization_barrier((t_low, to_mate, own))
    t_mate = rows_of_mate(to_mate)
    t_low_mate, t_low_other = rows_around(*edges(t_low, 3))
    update_here, t_low = lax.optimization_barrier((update_here, t_low))
    up_old, up_new = call(
        update_body, (laid, laid), lay_out_scratch(width), (update_here,), "lay_out_update", 9
    )
    t_high, up_new = lax.optimization_barrier((t_high, up_new))
    t_high_mate, t_high_other = rows_around(*edges(t_high, 3))
    h_first, h_last, t_low, t_high = lax.optimization_barrier((h_first, h_last, t_low, t_high))
    h_low, h_high = planes_around(h_first, h_last)
    face = call(
        corr_face_body, pairs["face"], [target_rows], (s_flat, t_low, t_high, t_mate, t_other), "face", 9, place
    )

    enc, enc_first, enc_last = call(
        corr_corner_body,
        (made(hidden.shape, BF16), two, two),
        [target_rows] + [pltpu.VMEM(pairs["corner"].shape, F32)],
        (s_flat, motion_here, small)
        + (own, face, t_low_mate, t_low_other, t_high_mate, t_high_other, wc),
        "corner",
        10,
        place,
    )
    e_low, e_high = planes_around(enc_first, enc_last)
    taps_head, enc = lax.optimization_barrier((jnp.transpose(w_head, (1, 0, 2)), enc))
    ca_old, ca_new, head = call(
        cand_body,
        (laid, laid, pltpu.HBM((32 * 8, width), BF16)),
        lay_out_scratch(width) + [pltpu.VMEM((32 * 8, LANES), F32)],
        (w_cand, taps_head),
        "lay_out_cand",
        9,
        from_hbm=(pltpu.VMEM,) * 2,
    )
    e_low, ca_new = lax.optimization_barrier((e_low, ca_new))
    h_low, h_high, enc = lax.optimization_barrier((h_low, h_high, enc))
    h_mate, h_other = rows_around(*rows_of(place, h_low, hidden_here, h_high, 2, "pack_hidden"))
    field = pltpu.VMEM((planes + 4, width, (rows + 4) * LANES), BF16)
    update_old, reset_old, near = call(
        old_body,
        (
            jax.ShapeDtypeStruct((planes, rows, width, cells), F32),
            jax.ShapeDtypeStruct((planes + 2, rows + 2, width, cells), F32),
            jax.ShapeDtypeStruct((planes + 2, width, (rows + 2) * LANES), BF16),
        ),
        [field],
        (hidden_here, small, h_low, h_high, h_mate, h_other, up_old, re_old),
        "old",
        10,
        place,
    )
    e_mate, e_other = rows_around(*rows_of(place, e_low, enc, e_high, 2, "pack_encoded"))

    ring = lambda n: jax.ShapeDtypeStruct((n, rows + 2, 8, cells), F32)
    ends = len(outer_planes(planes))
    part_low, part, part_high, e_field, gated, outer = call(
        gru_outer_body,
        (ring(1), ring(planes), ring(1), made(field.shape, BF16))
        + (made((planes + 2, width, (rows + 2) * LANES), BF16), made((ends, rows, width, cells), BF16)),
        [pltpu.VMEM((ends, width, wide), BF16)],
        (begun, small, near, update_old, reset_old, enc, e_low, e_high, e_mate, e_other)
        + (up_new, re_new, ca_old, ca_new, head),
        "gru_outer",
        12,
        place,
    )
    low, high = planes_around(part_low, part_high)
    state_out, part = call(
        gru_inner_body,
        (pltpu.HBM(hidden.shape, BF16), ring(planes)),
        [pltpu.VMEM((planes - ends, width, wide), BF16)],
        (small, near, update_old, e_field, gated, up_new, ca_old, ca_new, head, part, outer),
        "gru_inner",
        12,
    )
    row = jax.ShapeDtypeStruct((planes, 1, 8, cells), F32)
    mine, to_mate, to_other = call(
        mix_body,
        (jax.ShapeDtypeStruct((planes, rows, 8, cells), F32), row, row),
        [],
        (part, low, high),
        "mix",
        4,
        place,
    )
    mate, other = rows_around(to_mate, to_other)
    other = jnp.where(place[2] == 1, other, 0.0)
    odd = place[3] == 1
    below, above = jnp.where(odd, mate, other), jnp.where(odd, other, mate)
    row = lax.broadcasted_iota(jnp.int32, mine.shape, 1)
    total = mine + jnp.where(row == 0, below, 0.0) + jnp.where(row == rows - 1, above, 0.0)
    motion_out = total[:, :, : motion.shape[2]]
    return state_out, motion_out


def solution(mesh):
    split = P("gz", "gy", None, None)
    return jax.shard_map(
        on_device,
        mesh=mesh,
        in_specs=(split,) * 4 + (P(),) * 11,
        out_specs=(split, split),
        check_vma=False,
    )
```
